32 devices in a mesh: plane: 4 (over y, core), strip: 8 (over z, x).
Axes of the slice: x: 2, y: 2, z: 4, core: 2. Of those that a mesh axis runs over, the one named last changes fastest.
Arguments:
- u_field: bfloat16 [256, 64, 576], P('plane', 'strip'), may hold values from -6 to 6
- v_field: bfloat16 [256, 64, 576], P('plane', 'strip'), may hold values from -6 to 6
- sigma: float32 [256], P('plane'), may hold values from 1 to 3
- west: int32 [64, 16], P('strip'), may hold values from 0 to 15, each once within a row
- dinv: bfloat16 [64, 16, 1296], P('strip')
- west_coupling: bfloat16 [64, 16, 1296], P('strip'), may hold values from -0.28 to 0.28
- east_coupling: bfloat16 [64, 16, 1296], P('strip'), may hold values from -0.28 to 0.28
Outputs:
- u_out: bfloat16 [256, 64, 576], P('plane', 'strip')
- v_out: bfloat16 [256, 64, 576], P('plane', 'strip')
The draws below stay inside these ranges and needn't reach their ends.
Inputs may be any that keep to these rules, and one draw needn't show every extreme that they name: Each row of west is a permutation: every element of a column is the west neighbour of exactly one element of the next column.
All inputs are finite; a program needn't handle non-finite values.
Results may differ from the reference program's by a relative error of at most 0.001.
Values may be sent and summed in bfloat16 or wider, within the bound.
A program may use at most 64 MiB of HBM per device.

```python
import math
import jax
import jax.numpy as jnp
from jax import lax

Z = 256
NODES = 36
R = 16
NCT = 64


def draw_dinv(key, part):
    jitter = 0.1 * jax.random.normal(key, (NCT, R, NODES, NODES), jnp.float32)
    diagonal_part = 0.5 * jnp.eye(NODES, dtype=jnp.float32)
    return (diagonal_part[None, None, :, :] + jitter).reshape(NCT, R, NODES * NODES).astype(jnp.bfloat16)


def draw_west_coupling(key, part):
    subkey = jax.random.fold_in(key, 11)
    entries = jnp.clip(0.069 * jax.random.normal(subkey, (NCT, R, NODES * NODES), jnp.float32), -0.28, 0.28)
    return entries.astype(jnp.bfloat16)


def draw_east_coupling(key, part):
    subkey = jax.random.fold_in(key, 23)
    entries = jnp.clip(0.069 * jax.random.normal(subkey, (NCT, R, NODES * NODES), jnp.float32), -0.28, 0.28)
    return entries.astype(jnp.bfloat16)


def draw_sigma(key, part):
    subkey = jax.random.fold_in(key, 37)
    fraction = jax.random.uniform(subkey, (Z,), jnp.float32, 0.0, 1.0)
    highest = math.log(3.0)
    return jnp.exp(fraction * highest).astype(jnp.float32)


def block_levels(rng, shape, shards, low, largest):
    gain, own = 1.0, jax.random.fold_in(rng, 6)
    for position, parts in shards:
        heights = jnp.exp(jax.random.uniform(jax.random.fold_in(own, position), (parts,), jnp.float32, low / len(shards), largest / len(shards)))
        gain = gain * jnp.repeat(heights, shape[position] // parts).reshape([-1 if axis == position else 1 for axis in range(len(shape))])
    return gain


def normal_values(rng, shape, deviation, reach, split=(), kind=jnp.bfloat16):
    values = jax.random.normal(rng, shape, jnp.float32) * deviation
    if len(split) > 0:
        values = block_levels(rng, shape, split, -0.22, 0.18) * values
    return jnp.clip(values, min=-reach, max=reach).astype(kind)


def setup_inputs(seed: int = 0) -> dict:
    key_of = jax.random.split(jax.random.key(seed), 8)
    return {
        "u_field": normal_values(key_of[0], (Z, NCT, R * NODES), 1.0, 6.0, ((0, 4), (1, 8))),
        "v_field": normal_values(key_of[1], (Z, NCT, R * NODES), 1.0, 6.0, ((0, 4), (1, 8))),
        "sigma": draw_sigma(jax.random.fold_in(key_of[7], 71), 0),
        "west": jax.vmap(lambda own: jax.random.permutation(own, R))(jax.random.split(key_of[3], NCT)).reshape((NCT, R)).astype(jnp.int32),
        "dinv": draw_dinv(jax.random.fold_in(key_of[7], 71), 0),
        "west_coupling": draw_west_coupling(jax.random.fold_in(key_of[7], 71), 0),
        "east_coupling": draw_east_coupling(jax.random.fold_in(key_of[7], 71), 0),
    }


def fourier_tables(count):
    coeff_ids = jnp.arange(count, dtype=jnp.int32)
    plane_ids = jnp.arange(count, dtype=jnp.int32)
    wavenumber = (coeff_ids + 1) // 2
    steps_idx = (wavenumber[:, None] * plane_ids[None, :]) % count
    angles = steps_idx.astype(jnp.float32) * (2.0 * math.pi / count)
    is_sine = ((coeff_ids % 2) == 0) & (coeff_ids > 0)
    basis_rows = jnp.where(is_sine[:, None], jnp.sin(angles), jnp.cos(angles))
    edge_rows = (coeff_ids == 0) | (coeff_ids == count - 1)
    scaling = jnp.where(edge_rows, 1.0 / count, 2.0 / count).astype(jnp.float32)
    return basis_rows * scaling[:, None], basis_rows.T


def forward_strip(source, gains, inflow, inverse_blocks, west_blocks, onehots):
    def advance(previous, slices):
        source_col, inverse_col, west_col, onehot = slices
        shifted = jnp.einsum("rs,snl->rnl", onehot, previous, precision=lax.Precision.HIGHEST)
        west_term = jnp.einsum("rij,rjl->ril", west_col.astype(jnp.float32), shifted, precision=lax.Precision.HIGHEST)
        reduced = source_col - gains * west_term
        solved = jnp.einsum("rij,rjl->ril", inverse_col.astype(jnp.float32), reduced, precision=lax.Precision.HIGHEST)
        return solved, reduced
    return lax.scan(advance, inflow, (source, inverse_blocks, west_blocks, onehots))


def backward_strip(reduced_all, gains, inflow, inverse_blocks, east_blocks, onehots):
    def advance(east_term, slices):
        reduced_col, inverse_col, east_col, onehot = slices
        solved = jnp.einsum("rij,rjl->ril", inverse_col.astype(jnp.float32), reduced_col - gains * east_term, precision=lax.Precision.HIGHEST)
        east_part = jnp.einsum("rij,rjl->ril", east_col.astype(jnp.float32), solved, precision=lax.Precision.HIGHEST)
        routed = jnp.einsum("rs,ril->sil", onehot, east_part, precision=lax.Precision.HIGHEST)
        return routed, solved
    return lax.scan(advance, inflow, (reduced_all, inverse_blocks, east_blocks, onehots), reverse=True)


def reference(u_field, v_field, sigma, west, dinv, west_coupling, east_coupling):
    planes, total_cols, flat_width = u_field.shape
    elem_rows = flat_width // NODES
    forward_table, inverse_table = fourier_tables(planes)
    onehots = (west[:, :, None] == jnp.arange(elem_rows, dtype=jnp.int32)[None, None, :]).astype(jnp.float32)
    inverse_blocks = dinv.reshape(total_cols, elem_rows, NODES, NODES)
    west_blocks = west_coupling.reshape(total_cols, elem_rows, NODES, NODES)
    east_blocks = east_coupling.reshape(total_cols, elem_rows, NODES, NODES)

    def one_field(velocity):
        coeffs = jnp.einsum("kz,zcn->kcn", forward_table, velocity.astype(jnp.float32), precision=lax.Precision.HIGHEST)
        source = coeffs.reshape(planes, total_cols, elem_rows, NODES).transpose(1, 2, 3, 0)
        inflow = jnp.zeros((elem_rows, NODES, planes), jnp.float32)
        reduced_all = forward_strip(source, sigma, inflow, inverse_blocks, west_blocks, onehots)[1]
        solved_all = backward_strip(reduced_all, sigma, inflow, inverse_blocks, east_blocks, onehots)[1]
        result_modes = solved_all.transpose(3, 0, 1, 2).reshape(planes, total_cols, flat_width)
        return jnp.einsum("zk,kcn->zcn", inverse_table, result_modes, precision=lax.Precision.HIGHEST).astype(jnp.bfloat16)

    return (one_field(u_field), one_field(v_field))
```

```python
import math

import jax
import jax.numpy as jnp
import ml_dtypes
import numpy as np
from jax import lax
from jax.experimental import pallas as pl
from jax.experimental.pallas import tpu as pltpu
from jax.sharding import PartitionSpec as P

NODES = 36


def from_behind(block, axis, distance):
    devices = range(lax.axis_size(axis))
    route = [(i - distance, i) for i in devices if i - distance in devices]
    return lax.ppermute(block, axis, route)


def fourier_tables(count):
    coeff_ids = jnp.arange(count, dtype=jnp.int32)
    plane_ids = jnp.arange(count, dtype=jnp.int32)
    wavenumber = (coeff_ids + 1) // 2
    steps_idx = wavenumber[:, None] * plane_ids[None, :] % count
    angles = steps_idx.astype(jnp.float32) * (2.0 * math.pi / count)
    is_sine = (coeff_ids % 2 == 0) & (coeff_ids > 0)
    basis_rows = jnp.where(is_sine[:, None], jnp.sin(angles), jnp.cos(angles))
    edge_rows = (coeff_ids == 0) | (coeff_ids == count - 1)
    scaling = jnp.where(edge_rows, 1.0 / count, 2.0 / count).astype(jnp.float32)
    return (basis_rows * scaling[:, None], basis_rows.T)


def forward_strip(source, gains, inflow, inverse_blocks, west_blocks, onehots):

    def advance(previous, slices):
        source_col, inverse_col, west_col, onehot = slices
        shifted = jnp.einsum("rs,snl->rnl", onehot, previous, precision=lax.Precision.HIGHEST)
        west_term = jnp.einsum(
            "rij,rjl->ril", west_col.astype(jnp.float32), shifted, precision=lax.Precision.HIGHEST
        )
        reduced = source_col - gains * west_term
        solved = jnp.einsum(
            "rij,rjl->ril",
            inverse_col.astype(jnp.float32),
            reduced,
            precision=lax.Precision.HIGHEST,
        )
        return (solved, reduced)

    return lax.scan(advance, inflow, (source, inverse_blocks, west_blocks, onehots))


def backward_strip(reduced_all, gains, inflow, inverse_blocks, east_blocks, onehots):

    def advance(east_term, slices):
        reduced_col, inverse_col, east_col, onehot = slices
        solved = jnp.einsum(
            "rij,rjl->ril",
            inverse_col.astype(jnp.float32),
            reduced_col - gains * east_term,
            precision=lax.Precision.HIGHEST,
        )
        east_part = jnp.einsum(
            "rij,rjl->ril", east_col.astype(jnp.float32), solved, precision=lax.Precision.HIGHEST
        )
        routed = jnp.einsum("rs,ril->sil", onehot, east_part, precision=lax.Precision.HIGHEST)
        return (routed, solved)

    return lax.scan(
        advance, inflow, (reduced_all, inverse_blocks, east_blocks, onehots), reverse=True
    )


def run_chain(direction, block_count, advance, state, outgoing):
    strip_count = lax.axis_size("strip")
    strip_index = lax.axis_index("strip")
    turn_count = strip_count + block_count - 1

    def one_turn(step_turn, carry):
        incoming = from_behind(carry[0], "strip", direction)
        if direction > 0:
            position = step_turn - strip_index
        else:
            position = step_turn - (strip_count - 1 - strip_index)
        active = (position >= 0) & (position < block_count)
        lane_block = jnp.clip(position, 0, block_count - 1)

        def working(current):
            return advance(incoming, lane_block, current)

        def waiting(current):
            return current

        return lax.cond(active, working, waiting, carry)

    return lax.fori_loop(0, turn_count, one_turn, (outgoing, state))


def strip_chain_on_device(u_field, v_field, sigma, west, dinv, west_coupling, east_coupling):
    planes_dev, columns, flat_width = u_field.shape
    planes = planes_dev * lax.axis_size("plane")
    elem_rows = flat_width // NODES
    forward_table, inverse_table = fourier_tables(planes)
    pieces = (
        lax.all_to_all(u_field, "plane", split_axis=1, concat_axis=0, tiled=True),
        lax.all_to_all(v_field, "plane", split_axis=1, concat_axis=0, tiled=True),
    )
    spec_u, spec_v = tuple(
        (
            jnp.einsum(
                "kz,zcn->kcn",
                forward_table,
                piece.astype(jnp.float32),
                precision=lax.Precision.HIGHEST,
            )
            for piece in pieces
        )
    )
    mode_u, mode_v = (
        lax.all_to_all(spec_u, "plane", split_axis=0, concat_axis=1, tiled=True),
        lax.all_to_all(spec_v, "plane", split_axis=0, concat_axis=1, tiled=True),
    )
    modes_dev = mode_u.shape[0]
    lane_count = 2 * modes_dev
    stacked = (
        jnp.concatenate([mode_u, mode_v], 0)
        .reshape(lane_count, columns, elem_rows, NODES)
        .transpose(1, 2, 3, 0)
    )
    lane_gains = jnp.concatenate([sigma, sigma], 0)
    block_count = 1
    lane_width = lane_count // block_count
    onehots = (west[:, :, None] == jnp.arange(elem_rows, dtype=jnp.int32)[None, None, :]).astype(
        jnp.float32
    )
    inverse_blocks = dinv.reshape(columns, elem_rows, NODES, NODES)
    west_blocks = west_coupling.reshape(columns, elem_rows, NODES, NODES)
    east_blocks = east_coupling.reshape(columns, elem_rows, NODES, NODES)
    edge_zeros = jnp.zeros((elem_rows, NODES, lane_width), jnp.float32)

    def forward_advance(incoming, lane_block, carry):
        last_col, reduced = forward_strip(
            stacked, lane_gains, incoming, inverse_blocks, west_blocks, onehots
        )
        return (last_col, reduced)

    reduced_all = run_chain(1, block_count, forward_advance, jnp.zeros_like(stacked), edge_zeros)[1]

    def backward_advance(incoming, lane_block, carry):
        first_term, solved = backward_strip(
            reduced_all, lane_gains, incoming, inverse_blocks, east_blocks, onehots
        )
        return (first_term, solved)

    solved_all = run_chain(-1, block_count, backward_advance, jnp.zeros_like(stacked), edge_zeros)[
        1
    ]
    result_modes = solved_all.transpose(3, 0, 1, 2).reshape(lane_count, columns, flat_width)
    out_modes_u = result_modes[:modes_dev]
    out_modes_v = result_modes[modes_dev:]
    pieces = (
        lax.all_to_all(out_modes_u, "plane", split_axis=1, concat_axis=0, tiled=True),
        lax.all_to_all(out_modes_v, "plane", split_axis=1, concat_axis=0, tiled=True),
    )
    phys_u, phys_v = tuple(
        (
            jnp.einsum("zk,kcn->zcn", inverse_table, piece, precision=lax.Precision.HIGHEST).astype(
                jnp.bfloat16
            )
            for piece in pieces
        )
    )
    u_out, v_out = (
        lax.all_to_all(phys_u, "plane", split_axis=0, concat_axis=1, tiled=True),
        lax.all_to_all(phys_v, "plane", split_axis=0, concat_axis=1, tiled=True),
    )
    return (u_out, v_out)


PAD = 48


def split_table(table):
    high = table.astype(np.float32).astype(ml_dtypes.bfloat16)
    low = (table - high.astype(np.float64)).astype(ml_dtypes.bfloat16)
    return jnp.asarray(high), jnp.asarray(low)


def transform_tables(count, shares):
    ids = np.arange(count)
    angles = 2.0 * np.pi * (((ids[:, None] + 1) // 2 * ids[None, :]) % count) / count
    is_sine = (ids % 2 == 0) & (ids > 0)
    basis = np.where(is_sine[:, None], np.sin(angles), np.cos(angles))
    scaling = np.where((ids == 0) | (ids == count - 1), 1.0 / count, 2.0 / count)
    forward = basis * scaling[:, None]
    each = count // shares
    to_modes = np.zeros((shares, 2, each, 2, count))
    to_planes = np.zeros((2, count, shares, 2, each))
    for half in range(2):
        to_modes[:, half, :, half, :] = forward.T.reshape(shares, each, count)
        to_planes[half, :, :, half, :] = basis.reshape(count, shares, each)
    return (
        split_table(to_modes.reshape(2 * count, 2 * count)),
        split_table(to_planes.reshape(2 * count, 2 * count)),
    )


def split(value):
    high = value.astype(jnp.bfloat16)
    low = (value - high.astype(jnp.float32)).astype(jnp.bfloat16)
    return high, low


def dot(left, right):
    return jnp.dot(left, right, preferred_element_type=jnp.float32)


def label_kernel(onehot_ref, labels_ref):
    rows = onehot_ref.shape[1]
    first = lax.broadcasted_iota(jnp.int32, (rows, rows), 0)
    second = lax.broadcasted_iota(jnp.int32, (rows, rows), 1)

    def step(column, held):
        held = dot(onehot_ref[column], held).astype(jnp.bfloat16)
        labels_ref[column] = held
        return held

    lax.fori_loop(0, onehot_ref.shape[0], step, (first == second).astype(jnp.bfloat16))


def chain_kernel(
    shares, strips, half_cols,
    recv_ref, sigma_ref, inv_ref, west_ref, east_ref,
    fhi_ref, flo_ref, bhi_ref, blo_ref,
    out_ref, x_ref, a_ref, b_ref,
):
    columns = x_ref.shape[0]
    modes = x_ref.shape[2]
    lane = lax.broadcasted_iota(jnp.int32, (PAD, 3 * PAD), 1)

    def folded(left, right):
        high, low = split(dot(left, right))
        return jnp.where(lane < 2 * PAD, high.astype(jnp.float32), low.astype(jnp.float32)).astype(
            jnp.bfloat16
        )

    def prepare(column, carry):
        inverse = inv_ref[column][:, :PAD]
        a_ref[column] = folded(inverse, west_ref[column])
        b_ref[column] = folded(inverse, east_ref[jnp.minimum(column + 1, columns - 1)])
        return carry

    lax.fori_loop(0, columns, prepare, 0, unroll=4)

    def to_modes(strip, carry):
        planes = jnp.concatenate([recv_ref[share, strip] for share in range(shares)], axis=1)
        coeffs = dot(planes, fhi_ref[...]) + dot(planes, flo_ref[...])
        for half in range(2):
            for place in range(half_cols):
                own = coeffs[place * NODES : (place + 1) * NODES, half * modes : (half + 1) * modes]
                own = jnp.concatenate([own, jnp.zeros((PAD - NODES, modes), jnp.float32)], axis=0)
                high, low = split(own)
                column = (strip * 2 + half) * half_cols + place
                x_ref[column] = dot(inv_ref[column], jnp.concatenate([high, low], axis=0))
        return carry

    lax.fori_loop(0, strips, to_modes, 0)

    sigma = jnp.broadcast_to(sigma_ref[...], (PAD, modes))

    def stacked(value):
        high, low = split(value)
        return jnp.concatenate([high, low, high], axis=0)

    def forward(column, previous):
        value = x_ref[column] - sigma * dot(a_ref[column], stacked(previous))
        x_ref[column] = value
        return value

    last = lax.fori_loop(1, columns, forward, x_ref[0])

    def backward(step, following):
        column = columns - 2 - step
        value = x_ref[column] - sigma * dot(b_ref[column], stacked(following))
        x_ref[column] = value
        return value

    lax.fori_loop(0, columns - 1, backward, last)

    def to_planes(strip, carry):
        pieces = []
        for place in range(half_cols):
            first = x_ref[strip * 2 * half_cols + place]
            second = x_ref[(strip * 2 + 1) * half_cols + place]
            pieces.append(jnp.concatenate([first[:NODES], second[:NODES]], axis=1))
        high, low = split(jnp.concatenate(pieces, axis=0))
        planes = dot(high, bhi_ref[...]) + dot(low, bhi_ref[...]) + dot(high, blo_ref[...])
        width = planes.shape[1] // shares
        for share in range(shares):
            out_ref[share, strip] = planes[:, share * width : (share + 1) * width].astype(
                jnp.bfloat16
            )
        return carry

    lax.fori_loop(0, strips, to_planes, 0)


def chain_on_device(u_field, v_field, sigma, west, dinv, west_coupling, east_coupling):
    shares, strips = lax.axis_size("plane"), lax.axis_size("strip")
    planes_dev, columns, flat_width = u_field.shape
    planes = planes_dev * shares
    rows = flat_width // NODES
    half_cols = columns // 2
    groups = shares // 2
    all_columns = columns * strips
    vmem = pl.BlockSpec(memory_space=pltpu.VMEM)

    west_all = lax.all_gather(west, "strip", axis=0, tiled=True)
    sigma_all = lax.all_gather(sigma, "plane", axis=0, tiled=True)
    onehots = (west_all[:, :, None] == jnp.arange(rows, dtype=jnp.int32)).astype(jnp.bfloat16)
    labels_all = pl.pallas_call(
        label_kernel,
        out_shape=jax.ShapeDtypeStruct((all_columns, rows, rows), jnp.bfloat16),
        in_specs=[vmem],
        out_specs=vmem,
    )(onehots)
    labels = lax.dynamic_slice_in_dim(labels_all, lax.axis_index("strip") * columns, columns, 0)

    fields = jnp.stack([u_field, v_field]).reshape(2, planes_dev, columns, rows, NODES)
    outgoing = jnp.einsum("grc,fzgrn->gcfzn", labels, fields)
    outgoing = (
        outgoing.reshape(2, half_cols, groups, strips, 2, planes_dev, NODES)
        .transpose(2, 4, 3, 1, 6, 0, 5)
        .reshape(shares * strips, half_cols * NODES, 2 * planes_dev)
    )
    received = lax.all_to_all(outgoing, ("plane", "strip"), 0, 0, tiled=True)
    received = received.reshape(shares, strips, half_cols * NODES, 2 * planes_dev)

    group = lax.axis_index("plane") // 2
    own = lax.dynamic_slice_in_dim(labels, group * strips, strips, 2)
    matrices = jnp.stack([dinv, west_coupling, east_coupling])
    matrices = jnp.einsum("grc,mgre->cmge", own, matrices)
    matrices = lax.all_to_all(matrices, "strip", 0, 0, tiled=True)
    matrices = matrices.transpose(1, 0, 2, 3).reshape(3, all_columns, NODES, NODES)
    spare = PAD - NODES
    matrices = jnp.pad(matrices, ((0, 0), (0, 0), (0, spare), (0, spare)))
    inverse = jnp.concatenate([matrices[0]] * 2, axis=2)
    from_west = jnp.concatenate([matrices[1]] * 3, axis=2)
    from_east = jnp.concatenate([matrices[2]] * 3, axis=2)

    (fhi, flo), (bhi, blo) = transform_tables(planes, shares)
    result = pl.pallas_call(
        lambda *refs: chain_kernel(shares, strips, half_cols, *refs),
        out_shape=jax.ShapeDtypeStruct(received.shape, jnp.bfloat16),
        in_specs=[vmem] * 9,
        out_specs=vmem,
        scratch_shapes=[
            pltpu.VMEM((all_columns, PAD, planes), jnp.float32),
            pltpu.VMEM((all_columns, PAD, 3 * PAD), jnp.bfloat16),
            pltpu.VMEM((all_columns, PAD, 3 * PAD), jnp.bfloat16),
        ],
        compiler_params=pltpu.CompilerParams(vmem_limit_bytes=48 * 1024 * 1024),
    )(received, sigma_all.reshape(1, planes), inverse, from_west, from_east, fhi, flo, bhi, blo)

    returned = lax.all_to_all(
        result.reshape(shares * strips, half_cols * NODES, 2 * planes_dev),
        ("plane", "strip"), 0, 0, tiled=True,
    )
    returned = returned.reshape(groups, 2, strips, half_cols, NODES, 2, planes_dev)
    returned = returned.transpose(5, 3, 0, 2, 1, 6, 4).reshape(
        columns, rows, 2, planes_dev, NODES
    )
    outs = jnp.einsum("grc,gcfzn->fzgrn", labels, returned).reshape(
        2, planes_dev, columns, flat_width
    )
    return outs[0], outs[1]


def solution(mesh):
    in_specs = (
        P("plane", "strip", None),
        P("plane", "strip", None),
        P("plane"),
        P("strip", None),
        P("strip", None, None),
        P("strip", None, None),
        P("strip", None, None),
    )
    out_specs = (P("plane", "strip", None), P("plane", "strip", None))
    spread = mesh.shape["plane"] % 2 == 0 and mesh.shape["plane"] * mesh.shape["strip"] == 32
    body = chain_on_device if spread else strip_chain_on_device
    return jax.shard_map(
        body, mesh=mesh, in_specs=in_specs, out_specs=out_specs, check_vma=False
    )
```

```python
import math

import jax
import jax.numpy as jnp
import ml_dtypes
import numpy as np
from jax import lax
from jax.experimental import pallas as pl
from jax.experimental.pallas import tpu as pltpu
from jax.sharding import PartitionSpec as P

NODES = 36


def from_behind(block, axis, distance):
    devices = range(lax.axis_size(axis))
    route = [(i - distance, i) for i in devices if i - distance in devices]
    return lax.ppermute(block, axis, route)


def fourier_tables(count):
    coeff_ids = jnp.arange(count, dtype=jnp.int32)
    plane_ids = jnp.arange(count, dtype=jnp.int32)
    wavenumber = (coeff_ids + 1) // 2
    steps_idx = wavenumber[:, None] * plane_ids[None, :] % count
    angles = steps_idx.astype(jnp.float32) * (2.0 * math.pi / count)
    is_sine = (coeff_ids % 2 == 0) & (coeff_ids > 0)
    basis_rows = jnp.where(is_sine[:, None], jnp.sin(angles), jnp.cos(angles))
    edge_rows = (coeff_ids == 0) | (coeff_ids == count - 1)
    scaling = jnp.where(edge_rows, 1.0 / count, 2.0 / count).astype(jnp.float32)
    return (basis_rows * scaling[:, None], basis_rows.T)


def forward_strip(source, gains, inflow, inverse_blocks, west_blocks, onehots):

    def advance(previous, slices):
        source_col, inverse_col, west_col, onehot = slices
        shifted = jnp.einsum("rs,snl->rnl", onehot, previous, precision=lax.Precision.HIGHEST)
        west_term = jnp.einsum(
            "rij,rjl->ril", west_col.astype(jnp.float32), shifted, precision=lax.Precision.HIGHEST
        )
        reduced = source_col - gains * west_term
        solved = jnp.einsum(
            "rij,rjl->ril",
            inverse_col.astype(jnp.float32),
            reduced,
            precision=lax.Precision.HIGHEST,
        )
        return (solved, reduced)

    return lax.scan(advance, inflow, (source, inverse_blocks, west_blocks, onehots))


def backward_strip(reduced_all, gains, inflow, inverse_blocks, east_blocks, onehots):

    def advance(east_term, slices):
        reduced_col, inverse_col, east_col, onehot = slices
        solved = jnp.einsum(
            "rij,rjl->ril",
            inverse_col.astype(jnp.float32),
            reduced_col - gains * east_term,
            precision=lax.Precision.HIGHEST,
        )
        east_part = jnp.einsum(
            "rij,rjl->ril", east_col.astype(jnp.float32), solved, precision=lax.Precision.HIGHEST
        )
        routed = jnp.einsum("rs,ril->sil", onehot, east_part, precision=lax.Precision.HIGHEST)
        return (routed, solved)

    return lax.scan(
        advance, inflow, (reduced_all, inverse_blocks, east_blocks, onehots), reverse=True
    )


def run_chain(direction, block_count, advance, state, outgoing):
    strip_count = lax.axis_size("strip")
    strip_index = lax.axis_index("strip")
    turn_count = strip_count + block_count - 1

    def one_turn(step_turn, carry):
        incoming = from_behind(carry[0], "strip", direction)
        if direction > 0:
            position = step_turn - strip_index
        else:
            position = step_turn - (strip_count - 1 - strip_index)
        active = (position >= 0) & (position < block_count)
        lane_block = jnp.clip(position, 0, block_count - 1)

        def working(current):
            return advance(incoming, lane_block, current)

        def waiting(current):
            return current

        return lax.cond(active, working, waiting, carry)

    return lax.fori_loop(0, turn_count, one_turn, (outgoing, state))


def strip_chain_on_device(u_field, v_field, sigma, west, dinv, west_coupling, east_coupling):
    planes_dev, columns, flat_width = u_field.shape
    planes = planes_dev * lax.axis_size("plane")
    elem_rows = flat_width // NODES
    forward_table, inverse_table = fourier_tables(planes)
    pieces = (
        lax.all_to_all(u_field, "plane", split_axis=1, concat_axis=0, tiled=True),
        lax.all_to_all(v_field, "plane", split_axis=1, concat_axis=0, tiled=True),
    )
    spec_u, spec_v = tuple(
        (
            jnp.einsum(
                "kz,zcn->kcn",
                forward_table,
                piece.astype(jnp.float32),
                precision=lax.Precision.HIGHEST,
            )
            for piece in pieces
        )
    )
    mode_u, mode_v = (
        lax.all_to_all(spec_u, "plane", split_axis=0, concat_axis=1, tiled=True),
        lax.all_to_all(spec_v, "plane", split_axis=0, concat_axis=1, tiled=True),
    )
    modes_dev = mode_u.shape[0]
    lane_count = 2 * modes_dev
    stacked = (
        jnp.concatenate([mode_u, mode_v], 0)
        .reshape(lane_count, columns, elem_rows, NODES)
        .transpose(1, 2, 3, 0)
    )
    lane_gains = jnp.concatenate([sigma, sigma], 0)
    block_count = 1
    lane_width = lane_count // block_count
    onehots = (west[:, :, None] == jnp.arange(elem_rows, dtype=jnp.int32)[None, None, :]).astype(
        jnp.float32
    )
    inverse_blocks = dinv.reshape(columns, elem_rows, NODES, NODES)
    west_blocks = west_coupling.reshape(columns, elem_rows, NODES, NODES)
    east_blocks = east_coupling.reshape(columns, elem_rows, NODES, NODES)
    edge_zeros = jnp.zeros((elem_rows, NODES, lane_width), jnp.float32)

    def forward_advance(incoming, lane_block, carry):
        last_col, reduced = forward_strip(
            stacked, lane_gains, incoming, inverse_blocks, west_blocks, onehots
        )
        return (last_col, reduced)

    reduced_all = run_chain(1, block_count, forward_advance, jnp.zeros_like(stacked), edge_zeros)[1]

    def backward_advance(incoming, lane_block, carry):
        first_term, solved = backward_strip(
            reduced_all, lane_gains, incoming, inverse_blocks, east_blocks, onehots
        )
        return (first_term, solved)

    solved_all = run_chain(-1, block_count, backward_advance, jnp.zeros_like(stacked), edge_zeros)[
        1
    ]
    result_modes = solved_all.transpose(3, 0, 1, 2).reshape(lane_count, columns, flat_width)
    out_modes_u = result_modes[:modes_dev]
    out_modes_v = result_modes[modes_dev:]
    pieces = (
        lax.all_to_all(out_modes_u, "plane", split_axis=1, concat_axis=0, tiled=True),
        lax.all_to_all(out_modes_v, "plane", split_axis=1, concat_axis=0, tiled=True),
    )
    phys_u, phys_v = tuple(
        (
            jnp.einsum("zk,kcn->zcn", inverse_table, piece, precision=lax.Precision.HIGHEST).astype(
                jnp.bfloat16
            )
            for piece in pieces
        )
    )
    u_out, v_out = (
        lax.all_to_all(phys_u, "plane", split_axis=0, concat_axis=1, tiled=True),
        lax.all_to_all(phys_v, "plane", split_axis=0, concat_axis=1, tiled=True),
    )
    return (u_out, v_out)


PAD = 48


def split_table(table):
    high = table.astype(np.float32).astype(ml_dtypes.bfloat16)
    low = (table - high.astype(np.float64)).astype(ml_dtypes.bfloat16)
    return jnp.asarray(high), jnp.asarray(low)


def transform_tables(count, shares):
    ids = np.arange(count)
    angles = 2.0 * np.pi * (((ids[:, None] + 1) // 2 * ids[None, :]) % count) / count
    is_sine = (ids % 2 == 0) & (ids > 0)
    basis = np.where(is_sine[:, None], np.sin(angles), np.cos(angles))
    scaling = np.where((ids == 0) | (ids == count - 1), 1.0 / count, 2.0 / count)
    forward = basis * scaling[:, None]
    each = count // shares
    to_modes = np.zeros((shares, 2, each, 2, count))
    to_planes = np.zeros((2, count, shares, 2, each))
    for half in range(2):
        to_modes[:, half, :, half, :] = forward.T.reshape(shares, each, count)
        to_planes[half, :, :, half, :] = basis.reshape(count, shares, each)
    return (
        split_table(to_modes.reshape(2 * count, 2 * count)),
        split_table(to_planes.reshape(2 * count, 2 * count)),
    )


def split(value):
    high = value.astype(jnp.bfloat16)
    low = (value - high.astype(jnp.float32)).astype(jnp.bfloat16)
    return high, low


def dot(left, right):
    return jnp.dot(left, right, preferred_element_type=jnp.float32)


def label_kernel(
    onehot_ref, sigma_ref, labels_ref, sigmas_ref,
    local_ref, total_ref, totals_ref, strip_send, strip_recv, plane_send, plane_recv,
):
    columns, rows, _ = onehot_ref.shape
    shares, strips = sigmas_ref.shape[0], totals_ref.shape[0]
    my_share, my_strip = lax.axis_index("plane"), lax.axis_index("strip")

    barrier = pltpu.get_barrier_semaphore()
    for step in range(1, strips):
        pl.semaphore_signal(
            barrier, 1, device_id={"plane": my_share, "strip": (my_strip + step) % strips}
        )
    for step in range(1, shares):
        pl.semaphore_signal(
            barrier, 1, device_id={"plane": (my_share + step) % shares, "strip": my_strip}
        )

    start = (
        lax.broadcasted_iota(jnp.int32, (rows, 128), 0)
        == lax.broadcasted_iota(jnp.int32, (rows, 128), 1)
    ).astype(jnp.bfloat16)
    held = start
    for column in range(columns):
        held = dot(onehot_ref[column], held).astype(jnp.bfloat16)
        local_ref[column] = held
    total_ref[...] = held
    pl.semaphore_wait(barrier, strips + shares - 2)

    def strip_copy(step, slot):
        return pltpu.make_async_remote_copy(
            src_ref=total_ref,
            dst_ref=totals_ref.at[slot],
            send_sem=strip_send.at[step],
            recv_sem=strip_recv.at[slot],
            device_id={"plane": my_share, "strip": (my_strip + step) % strips},
        )

    def plane_copy(step, slot):
        return pltpu.make_async_remote_copy(
            src_ref=sigma_ref,
            dst_ref=sigmas_ref.at[slot],
            send_sem=plane_send.at[step],
            recv_sem=plane_recv.at[slot],
            device_id={"plane": (my_share + step) % shares, "strip": my_strip},
        )

    for step in range(1, strips):
        strip_copy(step, my_strip).start()
    for step in range(1, shares):
        plane_copy(step, my_share).start()
    totals_ref[my_strip] = held
    sigmas_ref[my_share] = sigma_ref[...]
    for step in range(1, strips):
        strip_copy(step, (my_strip + strips - step) % strips).wait_recv()
    before = start
    for strip in range(strips - 1):
        joined = dot(totals_ref[strip][:, :rows], before)
        before = jnp.where(strip < my_strip, joined, before.astype(jnp.float32)).astype(
            jnp.bfloat16
        )
    for column in range(columns):
        labels_ref[column] = dot(local_ref[column][:, :rows], before).astype(jnp.bfloat16)
    for step in range(1, shares):
        plane_copy(step, (my_share + shares - step) % shares).wait_recv()
    for step in range(1, strips):
        strip_copy(step, my_strip).wait_send()
    for step in range(1, shares):
        plane_copy(step, my_share).wait_send()


def chain_kernel(
    shares, strips, half_cols,
    recv_ref, sigma_ref, inv_ref, west_ref, east_ref,
    fhi_ref, flo_ref, bhi_ref, blo_ref,
    out_ref, x_ref, a_ref, b_ref, planes_ref, send_sems, recv_sems, own_sem,
):
    my_share, my_strip = lax.axis_index("plane"), lax.axis_index("strip")
    me = my_share * strips + my_strip
    devices = shares * strips

    barrier = pltpu.get_barrier_semaphore()

    def greet(step, carry):
        other = (me + step) % devices
        pl.semaphore_signal(
            barrier, 1, device_id={"plane": other // strips, "strip": other % strips}
        )
        return carry

    lax.fori_loop(1, devices, greet, 0)

    def result_copy(share, strip, slot):
        return pltpu.make_async_remote_copy(
            src_ref=planes_ref.at[share * strips + strip],
            dst_ref=out_ref.at[slot],
            send_sem=send_sems.at[share * strips + strip],
            recv_sem=recv_sems.at[slot],
            device_id={"plane": share, "strip": strip},
        )

    columns = x_ref.shape[0]
    modes = x_ref.shape[2]
    lane = lax.broadcasted_iota(jnp.int32, (PAD, 3 * PAD), 1)

    def folded(left, right):
        high, low = split(dot(left, right))
        return jnp.where(lane < 2 * PAD, high.astype(jnp.float32), low.astype(jnp.float32)).astype(
            jnp.bfloat16
        )

    def prepare(column, carry):
        inverse = inv_ref[column][:, :PAD]
        a_ref[column] = folded(inverse, west_ref[column])
        b_ref[column] = folded(inverse, east_ref[jnp.minimum(column + 1, columns - 1)])
        return carry

    lax.fori_loop(0, columns, prepare, 0, unroll=4)

    sigma = jnp.broadcast_to(sigma_ref[...], (PAD, modes))

    def stacked(value):
        high, low = split(value)
        return jnp.concatenate([high, low, high], axis=0)

    def forward(strip, previous):
        planes = jnp.concatenate([recv_ref[share, strip] for share in range(shares)], axis=1)
        coeffs = dot(planes, fhi_ref[...]) + dot(planes, flo_ref[...])
        sources = []
        for half in range(2):
            for place in range(half_cols):
                own = coeffs[place * NODES : (place + 1) * NODES, half * modes : (half + 1) * modes]
                own = jnp.concatenate([own, jnp.zeros((PAD - NODES, modes), jnp.float32)], axis=0)
                high, low = split(own)
                column = (strip * 2 + half) * half_cols + place
                sources.append(dot(inv_ref[column], jnp.concatenate([high, low], axis=0)))
        for place in range(2 * half_cols):
            column = strip * 2 * half_cols + place
            previous = sources[place] - sigma * dot(a_ref[column], stacked(previous))
            x_ref[column] = previous
        return previous

    nothing = jnp.zeros((PAD, modes), jnp.float32)
    lax.fori_loop(0, strips, forward, nothing)
    pl.semaphore_wait(barrier, devices - 1)

    def backward(step, following):
        strip = strips - 1 - step
        solved = [None] * (2 * half_cols)
        for place in reversed(range(2 * half_cols)):
            column = strip * 2 * half_cols + place
            following = x_ref[column] - sigma * dot(b_ref[column], stacked(following))
            solved[place] = following
        pieces = [
            jnp.concatenate([solved[place][:NODES], solved[half_cols + place][:NODES]], axis=1)
            for place in range(half_cols)
        ]
        high, low = split(jnp.concatenate(pieces, axis=0))
        planes = dot(high, bhi_ref[...]) + dot(low, bhi_ref[...]) + dot(high, blo_ref[...])
        width = planes.shape[1] // shares
        for share in range(shares):
            planes_ref[share * strips + strip] = planes[
                :, share * width : (share + 1) * width
            ].astype(jnp.bfloat16)
        for share in range(shares):
            mine = (share == my_share) & (strip == my_strip)

            @pl.when(jnp.logical_not(mine))
            def _():
                result_copy(share, strip, me).start()

        return following

    lax.fori_loop(0, strips, backward, nothing)
    own_copy = pltpu.make_async_copy(planes_ref.at[me], out_ref.at[me], own_sem)
    own_copy.start()
    own_copy.wait()

    def finish(step, carry):
        source = (me + step) % devices
        result_copy(source // strips, source % strips, source).wait_recv()
        result_copy(source // strips, source % strips, me).wait_send()
        return carry

    lax.fori_loop(1, devices, finish, 0)


def chain_on_device(u_field, v_field, sigma, west, dinv, west_coupling, east_coupling):
    shares, strips = lax.axis_size("plane"), lax.axis_size("strip")
    planes_dev, columns, flat_width = u_field.shape
    planes = planes_dev * shares
    rows = flat_width // NODES
    half_cols = columns // 2
    groups = shares // 2
    all_columns = columns * strips
    vmem = pl.BlockSpec(memory_space=pltpu.VMEM)

    onehots = (west[:, :, None] == jnp.arange(rows, dtype=jnp.int32)).astype(jnp.bfloat16)
    sigma_tile = jnp.broadcast_to(jnp.pad(sigma, (0, 128 - planes_dev))[None], (8, 128))
    labels, sigma_tiles = pl.pallas_call(
        label_kernel,
        out_shape=(
            jax.ShapeDtypeStruct((columns, rows, 128), jnp.bfloat16),
            jax.ShapeDtypeStruct((shares, 8, 128), jnp.float32),
        ),
        in_specs=[vmem] * 2,
        out_specs=(vmem, vmem),
        scratch_shapes=[
            pltpu.VMEM((columns, rows, 128), jnp.bfloat16),
            pltpu.VMEM((rows, 128), jnp.bfloat16),
            pltpu.VMEM((strips, rows, 128), jnp.bfloat16),
            pltpu.SemaphoreType.DMA((strips,)),
            pltpu.SemaphoreType.DMA((strips,)),
            pltpu.SemaphoreType.DMA((shares,)),
            pltpu.SemaphoreType.DMA((shares,)),
        ],
        compiler_params=pltpu.CompilerParams(collective_id=0, has_side_effects=True),
    )(onehots, sigma_tile)
    labels = labels[:, :, :rows]
    sigma_all = sigma_tiles[:, 0, :planes_dev].reshape(planes)

    fields = jnp.stack([u_field, v_field]).reshape(2, planes_dev, columns, rows, NODES)
    outgoing = jnp.einsum("grc,fzgrn->gcfzn", labels, fields)
    outgoing = (
        outgoing.reshape(2, half_cols, groups, strips, 2, planes_dev, NODES)
        .transpose(2, 4, 3, 1, 6, 0, 5)
        .reshape(shares * strips, half_cols * NODES, 2 * planes_dev)
    )
    received = lax.all_to_all(outgoing, ("plane", "strip"), 0, 0, tiled=True)
    received = received.reshape(shares, strips, half_cols * NODES, 2 * planes_dev)

    group = lax.axis_index("plane") // 2
    own = lax.dynamic_slice_in_dim(labels, group * strips, strips, 2)
    matrices = jnp.stack([dinv, west_coupling, east_coupling])
    matrices = jnp.einsum("grc,mgre->cmge", own, matrices)
    matrices = lax.all_to_all(matrices, "strip", 0, 0, tiled=True)
    matrices = matrices.transpose(1, 0, 2, 3).reshape(3, all_columns, NODES, NODES)
    spare = PAD - NODES
    matrices = jnp.pad(matrices, ((0, 0), (0, 0), (0, spare), (0, spare)))
    inverse = jnp.concatenate([matrices[0]] * 2, axis=2)
    from_west = jnp.concatenate([matrices[1]] * 3, axis=2)
    from_east = jnp.concatenate([matrices[2]] * 3, axis=2)

    (fhi, flo), (bhi, blo) = transform_tables(planes, shares)
    result = pl.pallas_call(
        lambda *refs: chain_kernel(shares, strips, half_cols, *refs),
        out_shape=jax.ShapeDtypeStruct(outgoing.shape, jnp.bfloat16),
        in_specs=[vmem] * 9,
        out_specs=vmem,
        scratch_shapes=[
            pltpu.VMEM((all_columns, PAD, planes), jnp.float32),
            pltpu.VMEM((all_columns, PAD, 3 * PAD), jnp.bfloat16),
            pltpu.VMEM((all_columns, PAD, 3 * PAD), jnp.bfloat16),
            pltpu.VMEM(outgoing.shape, jnp.bfloat16),
            pltpu.SemaphoreType.DMA((shares * strips,)),
            pltpu.SemaphoreType.DMA((shares * strips,)),
            pltpu.SemaphoreType.DMA,
        ],
        compiler_params=pltpu.CompilerParams(
            vmem_limit_bytes=48 * 1024 * 1024, collective_id=1, has_side_effects=True
        ),
    )(received, sigma_all.reshape(1, planes), inverse, from_west, from_east, fhi, flo, bhi, blo)

    returned = result.reshape(groups, 2, strips, half_cols, NODES, 2, planes_dev)
    returned = returned.transpose(5, 3, 0, 2, 1, 6, 4).reshape(
        columns, rows, 2, planes_dev, NODES
    )
    outs = jnp.einsum("grc,gcfzn->fzgrn", labels, returned).reshape(
        2, planes_dev, columns, flat_width
    )
    return outs[0], outs[1]


def solution(mesh):
    in_specs = (
        P("plane", "strip", None),
        P("plane", "strip", None),
        P("plane"),
        P("strip", None),
        P("strip", None, None),
        P("strip", None, None),
        P("strip", None, None),
    )
    out_specs = (P("plane", "strip", None), P("plane", "strip", None))
    spread = mesh.shape["plane"] % 2 == 0 and mesh.shape["plane"] * mesh.shape["strip"] == 32
    body = chain_on_device if spread else strip_chain_on_device
    return jax.shard_map(
        body, mesh=mesh, in_specs=in_specs, out_specs=out_specs, check_vma=False
    )
```

```python
import math

import jax
import jax.numpy as jnp
import ml_dtypes
import numpy as np
from jax import lax
from jax.experimental import pallas as pl
from jax.experimental.pallas import tpu as pltpu
from jax.sharding import PartitionSpec as P

NODES = 36


def from_behind(block, axis, distance):
    devices = range(lax.axis_size(axis))
    route = [(i - distance, i) for i in devices if i - distance in devices]
    return lax.ppermute(block, axis, route)


def fourier_tables(count):
    coeff_ids = jnp.arange(count, dtype=jnp.int32)
    plane_ids = jnp.arange(count, dtype=jnp.int32)
    wavenumber = (coeff_ids + 1) // 2
    steps_idx = wavenumber[:, None] * plane_ids[None, :] % count
    angles = steps_idx.astype(jnp.float32) * (2.0 * math.pi / count)
    is_sine = (coeff_ids % 2 == 0) & (coeff_ids > 0)
    basis_rows = jnp.where(is_sine[:, None], jnp.sin(angles), jnp.cos(angles))
    edge_rows = (coeff_ids == 0) | (coeff_ids == count - 1)
    scaling = jnp.where(edge_rows, 1.0 / count, 2.0 / count).astype(jnp.float32)
    return (basis_rows * scaling[:, None], basis_rows.T)


def forward_strip(source, gains, inflow, inverse_blocks, west_blocks, onehots):

    def advance(previous, slices):
        source_col, inverse_col, west_col, onehot = slices
        shifted = jnp.einsum("rs,snl->rnl", onehot, previous, precision=lax.Precision.HIGHEST)
        west_term = jnp.einsum(
            "rij,rjl->ril", west_col.astype(jnp.float32), shifted, precision=lax.Precision.HIGHEST
        )
        reduced = source_col - gains * west_term
        solved = jnp.einsum(
            "rij,rjl->ril",
            inverse_col.astype(jnp.float32),
            reduced,
            precision=lax.Precision.HIGHEST,
        )
        return (solved, reduced)

    return lax.scan(advance, inflow, (source, inverse_blocks, west_blocks, onehots))


def backward_strip(reduced_all, gains, inflow, inverse_blocks, east_blocks, onehots):

    def advance(east_term, slices):
        reduced_col, inverse_col, east_col, onehot = slices
        solved = jnp.einsum(
            "rij,rjl->ril",
            inverse_col.astype(jnp.float32),
            reduced_col - gains * east_term,
            precision=lax.Precision.HIGHEST,
        )
        east_part = jnp.einsum(
            "rij,rjl->ril", east_col.astype(jnp.float32), solved, precision=lax.Precision.HIGHEST
        )
        routed = jnp.einsum("rs,ril->sil", onehot, east_part, precision=lax.Precision.HIGHEST)
        return (routed, solved)

    return lax.scan(
        advance, inflow, (reduced_all, inverse_blocks, east_blocks, onehots), reverse=True
    )


def run_chain(direction, block_count, advance, state, outgoing):
    strip_count = lax.axis_size("strip")
    strip_index = lax.axis_index("strip")
    turn_count = strip_count + block_count - 1

    def one_turn(step_turn, carry):
        incoming = from_behind(carry[0], "strip", direction)
        if direction > 0:
            position = step_turn - strip_index
        else:
            position = step_turn - (strip_count - 1 - strip_index)
        active = (position >= 0) & (position < block_count)
        lane_block = jnp.clip(position, 0, block_count - 1)

        def working(current):
            return advance(incoming, lane_block, current)

        def waiting(current):
            return current

        return lax.cond(active, working, waiting, carry)

    return lax.fori_loop(0, turn_count, one_turn, (outgoing, state))


def strip_chain_on_device(u_field, v_field, sigma, west, dinv, west_coupling, east_coupling):
    planes_dev, columns, flat_width = u_field.shape
    planes = planes_dev * lax.axis_size("plane")
    elem_rows = flat_width // NODES
    forward_table, inverse_table = fourier_tables(planes)
    pieces = (
        lax.all_to_all(u_field, "plane", split_axis=1, concat_axis=0, tiled=True),
        lax.all_to_all(v_field, "plane", split_axis=1, concat_axis=0, tiled=True),
    )
    spec_u, spec_v = tuple(
        (
            jnp.einsum(
                "kz,zcn->kcn",
                forward_table,
                piece.astype(jnp.float32),
                precision=lax.Precision.HIGHEST,
            )
            for piece in pieces
        )
    )
    mode_u, mode_v = (
        lax.all_to_all(spec_u, "plane", split_axis=0, concat_axis=1, tiled=True),
        lax.all_to_all(spec_v, "plane", split_axis=0, concat_axis=1, tiled=True),
    )
    modes_dev = mode_u.shape[0]
    lane_count = 2 * modes_dev
    stacked = (
        jnp.concatenate([mode_u, mode_v], 0)
        .reshape(lane_count, columns, elem_rows, NODES)
        .transpose(1, 2, 3, 0)
    )
    lane_gains = jnp.concatenate([sigma, sigma], 0)
    block_count = 1
    lane_width = lane_count // block_count
    onehots = (west[:, :, None] == jnp.arange(elem_rows, dtype=jnp.int32)[None, None, :]).astype(
        jnp.float32
    )
    inverse_blocks = dinv.reshape(columns, elem_rows, NODES, NODES)
    west_blocks = west_coupling.reshape(columns, elem_rows, NODES, NODES)
    east_blocks = east_coupling.reshape(columns, elem_rows, NODES, NODES)
    edge_zeros = jnp.zeros((elem_rows, NODES, lane_width), jnp.float32)

    def forward_advance(incoming, lane_block, carry):
        last_col, reduced = forward_strip(
            stacked, lane_gains, incoming, inverse_blocks, west_blocks, onehots
        )
        return (last_col, reduced)

    reduced_all = run_chain(1, block_count, forward_advance, jnp.zeros_like(stacked), edge_zeros)[1]

    def backward_advance(incoming, lane_block, carry):
        first_term, solved = backward_strip(
            reduced_all, lane_gains, incoming, inverse_blocks, east_blocks, onehots
        )
        return (first_term, solved)

    solved_all = run_chain(-1, block_count, backward_advance, jnp.zeros_like(stacked), edge_zeros)[
        1
    ]
    result_modes = solved_all.transpose(3, 0, 1, 2).reshape(lane_count, columns, flat_width)
    out_modes_u = result_modes[:modes_dev]
    out_modes_v = result_modes[modes_dev:]
    pieces = (
        lax.all_to_all(out_modes_u, "plane", split_axis=1, concat_axis=0, tiled=True),
        lax.all_to_all(out_modes_v, "plane", split_axis=1, concat_axis=0, tiled=True),
    )
    phys_u, phys_v = tuple(
        (
            jnp.einsum("zk,kcn->zcn", inverse_table, piece, precision=lax.Precision.HIGHEST).astype(
                jnp.bfloat16
            )
            for piece in pieces
        )
    )
    u_out, v_out = (
        lax.all_to_all(phys_u, "plane", split_axis=0, concat_axis=1, tiled=True),
        lax.all_to_all(phys_v, "plane", split_axis=0, concat_axis=1, tiled=True),
    )
    return (u_out, v_out)


PAD = 48


def split_table(table):
    high = table.astype(np.float32).astype(ml_dtypes.bfloat16)
    low = (table - high.astype(np.float64)).astype(ml_dtypes.bfloat16)
    return jnp.asarray(high), jnp.asarray(low)


def transform_tables(count, shares):
    ids = np.arange(count)
    angles = 2.0 * np.pi * (((ids[:, None] + 1) // 2 * ids[None, :]) % count) / count
    is_sine = (ids % 2 == 0) & (ids > 0)
    basis = np.where(is_sine[:, None], np.sin(angles), np.cos(angles))
    scaling = np.where((ids == 0) | (ids == count - 1), 1.0 / count, 2.0 / count)
    forward = basis * scaling[:, None]
    each = count // shares
    to_modes = np.zeros((shares, 2, each, 2, count))
    to_planes = np.zeros((2, count, shares, 2, each))
    for half in range(2):
        to_modes[:, half, :, half, :] = forward.T.reshape(shares, each, count)
        to_planes[half, :, :, half, :] = basis.reshape(count, shares, each)
    return (
        split_table(to_modes.reshape(2 * count, 2 * count)),
        split_table(to_planes.reshape(2 * count, 2 * count)),
    )


def split(value):
    high = value.astype(jnp.bfloat16)
    low = (value - high.astype(jnp.float32)).astype(jnp.bfloat16)
    return high, low


def dot(left, right):
    return jnp.dot(left, right, preferred_element_type=jnp.float32)


def label_kernel(
    onehot_ref, sigma_ref, labels_ref, sigmas_ref,
    local_ref, total_ref, totals_ref, strip_send, strip_recv, plane_send, plane_recv,
):
    columns, rows, _ = onehot_ref.shape
    shares, strips = sigmas_ref.shape[0], totals_ref.shape[0]
    my_share, my_strip = lax.axis_index("plane"), lax.axis_index("strip")

    barrier = pltpu.get_barrier_semaphore()
    for step in range(1, strips):
        pl.semaphore_signal(
            barrier, 1, device_id={"plane": my_share, "strip": (my_strip + step) % strips}
        )
    for step in range(1, shares):
        pl.semaphore_signal(
            barrier, 1, device_id={"plane": (my_share + step) % shares, "strip": my_strip}
        )

    start = (
        lax.broadcasted_iota(jnp.int32, (rows, 128), 0)
        == lax.broadcasted_iota(jnp.int32, (rows, 128), 1)
    ).astype(jnp.bfloat16)
    held = start
    for column in range(columns):
        held = dot(onehot_ref[column], held).astype(jnp.bfloat16)
        local_ref[column] = held
    total_ref[...] = held
    pl.semaphore_wait(barrier, strips + shares - 2)

    def strip_copy(step, slot):
        return pltpu.make_async_remote_copy(
            src_ref=total_ref,
            dst_ref=totals_ref.at[slot],
            send_sem=strip_send.at[step],
            recv_sem=strip_recv.at[slot],
            device_id={"plane": my_share, "strip": (my_strip + step) % strips},
        )

    def plane_copy(step, slot):
        return pltpu.make_async_remote_copy(
            src_ref=sigma_ref,
            dst_ref=sigmas_ref.at[slot],
            send_sem=plane_send.at[step],
            recv_sem=plane_recv.at[slot],
            device_id={"plane": (my_share + step) % shares, "strip": my_strip},
        )

    for step in range(1, strips):
        strip_copy(step, my_strip).start()
    for step in range(1, shares):
        plane_copy(step, my_share).start()
    totals_ref[my_strip] = held
    sigmas_ref[my_share] = sigma_ref[...]
    for step in range(1, strips):
        strip_copy(step, (my_strip + strips - step) % strips).wait_recv()
    before = start
    for strip in range(strips - 1):
        joined = dot(totals_ref[strip][:, :rows], before)
        before = jnp.where(strip < my_strip, joined, before.astype(jnp.float32)).astype(
            jnp.bfloat16
        )
    for column in range(columns):
        labels_ref[column] = dot(local_ref[column][:, :rows], before).astype(jnp.bfloat16)
    for step in range(1, shares):
        plane_copy(step, (my_share + shares - step) % shares).wait_recv()
    for step in range(1, strips):
        strip_copy(step, my_strip).wait_send()
    for step in range(1, shares):
        plane_copy(step, my_share).wait_send()


def chain_kernel(
    shares, strips, half_cols,
    source_ref, sigma_ref, flat_ref, fhi_in, flo_in, bhi_in, blo_in,
    out_ref,
    x_ref, a_ref, b_ref, inv_ref, square_ref, recv_ref, planes_ref,
    fhi_ref, flo_ref, bhi_ref, blo_ref,
    first_send, first_recv, send_sems, recv_sems, own_sem, table_sems,
):
    my_share, my_strip = lax.axis_index("plane"), lax.axis_index("strip")
    me = my_share * strips + my_strip
    devices = shares * strips
    tables = [
        pltpu.make_async_copy(given, kept, table_sems.at[place])
        for place, (given, kept) in enumerate(
            [(fhi_in, fhi_ref), (flo_in, flo_ref), (bhi_in, bhi_ref), (blo_in, blo_ref)]
        )
    ]
    own_source = pltpu.make_async_copy(source_ref.at[me], recv_ref.at[me], own_sem)
    own_source.start()
    for table in tables:
        table.start()

    barrier = pltpu.get_barrier_semaphore()

    def greet(step, carry):
        other = (me + step) % devices
        pl.semaphore_signal(
            barrier, 1, device_id={"plane": other // strips, "strip": other % strips}
        )
        return carry

    lax.fori_loop(1, devices, greet, 0)

    pl.semaphore_wait(barrier, devices - 1)

    def source_copy(other, slot):
        return pltpu.make_async_remote_copy(
            src_ref=source_ref.at[other],
            dst_ref=recv_ref.at[slot],
            send_sem=first_send.at[other],
            recv_sem=first_recv.at[slot],
            device_id={"plane": other // strips, "strip": other % strips},
        )

    def send_source(step, carry):
        source_copy((me + step) % devices, me).start()
        return carry

    lax.fori_loop(1, devices, send_source, 0)

    def result_copy(share, strip, slot):
        return pltpu.make_async_remote_copy(
            src_ref=planes_ref.at[share * strips + strip],
            dst_ref=out_ref.at[slot],
            send_sem=send_sems.at[share * strips + strip],
            recv_sem=recv_sems.at[slot],
            device_id={"plane": share, "strip": strip},
        )

    columns = x_ref.shape[0]
    modes = x_ref.shape[2]
    per_strip = 2 * half_cols
    square_ref[...] = jnp.zeros_like(square_ref)

    def unflatten(strip, carry):
        flat = flat_ref[strip].astype(jnp.float32)
        for row in range(NODES):
            square_ref[strip, :, row, :NODES] = flat[:, row * NODES : (row + 1) * NODES]
        return carry

    lax.fori_loop(0, strips, unflatten, 0)

    def repeated(count):
        row = lax.broadcasted_iota(jnp.int32, (PAD, count * PAD), 0)
        lane = lax.broadcasted_iota(jnp.int32, (PAD, count * PAD), 1)
        return (row == lane % PAD).astype(jnp.bfloat16)

    lane = lax.broadcasted_iota(jnp.int32, (PAD, 3 * PAD), 1)
    twice, thrice = repeated(2), repeated(3)

    def block(kind, column):
        strip, place = column // per_strip, column % per_strip
        return square_ref[strip, kind * per_strip + place][:, :PAD].astype(jnp.bfloat16)

    def folded(left, right):
        right = dot(right, thrice).astype(jnp.bfloat16)
        high, low = split(dot(left, right))
        return jnp.where(lane < 2 * PAD, high.astype(jnp.float32), low.astype(jnp.float32)).astype(
            jnp.bfloat16
        )

    def prepare(column, carry):
        inverse = block(0, column)
        inv_ref[column] = dot(inverse, twice).astype(jnp.bfloat16)
        a_ref[column] = folded(inverse, block(1, column))
        b_ref[column] = folded(inverse, block(2, jnp.minimum(column + 1, columns - 1)))
        return carry

    lax.fori_loop(0, columns, prepare, 0, unroll=4)

    sigma = jnp.broadcast_to(sigma_ref[...], (PAD, modes))

    def stacked(value):
        high, low = split(value)
        return jnp.concatenate([high, low, high], axis=0)

    def forward(strip, previous):
        for share in range(shares):

            @pl.when(share * strips + strip != me)
            def _():
                source_copy(me, share * strips + strip).wait_recv()

        planes = jnp.concatenate(
            [recv_ref[share * strips + strip] for share in range(shares)], axis=1
        )
        coeffs = dot(planes, fhi_ref[...]) + dot(planes, flo_ref[...])
        sources = []
        for half in range(2):
            for place in range(half_cols):
                own = coeffs[place * NODES : (place + 1) * NODES, half * modes : (half + 1) * modes]
                own = jnp.concatenate([own, jnp.zeros((PAD - NODES, modes), jnp.float32)], axis=0)
                high, low = split(own)
                column = (strip * 2 + half) * half_cols + place
                sources.append(dot(inv_ref[column], jnp.concatenate([high, low], axis=0)))
        for place in range(2 * half_cols):
            column = strip * 2 * half_cols + place
            previous = sources[place] - sigma * dot(a_ref[column], stacked(previous))
            x_ref[column] = previous
        return previous

    nothing = jnp.zeros((PAD, modes), jnp.float32)
    own_source.wait()
    for table in tables:
        table.wait()
    lax.fori_loop(0, strips, forward, nothing)

    def backward(step, following):
        strip = strips - 1 - step
        solved = [None] * (2 * half_cols)
        for place in reversed(range(2 * half_cols)):
            column = strip * 2 * half_cols + place
            following = x_ref[column] - sigma * dot(b_ref[column], stacked(following))
            solved[place] = following
        pieces = [
            jnp.concatenate([solved[place][:NODES], solved[half_cols + place][:NODES]], axis=1)
            for place in range(half_cols)
        ]
        high, low = split(jnp.concatenate(pieces, axis=0))
        planes = dot(high, bhi_ref[...]) + dot(low, bhi_ref[...]) + dot(high, blo_ref[...])
        width = planes.shape[1] // shares
        for share in range(shares):
            planes_ref[share * strips + strip] = planes[
                :, share * width : (share + 1) * width
            ].astype(jnp.bfloat16)
        for share in range(shares):
            mine = (share == my_share) & (strip == my_strip)

            @pl.when(jnp.logical_not(mine))
            def _():
                result_copy(share, strip, me).start()

        return following

    lax.fori_loop(0, strips, backward, nothing)
    own_copy = pltpu.make_async_copy(planes_ref.at[me], out_ref.at[me], own_sem)
    own_copy.start()
    own_copy.wait()

    def finish(step, carry):
        source = (me + step) % devices
        result_copy(source // strips, source % strips, source).wait_recv()
        result_copy(source // strips, source % strips, me).wait_send()
        source_copy(source, me).wait_send()
        return carry

    lax.fori_loop(1, devices, finish, 0)


def chain_on_device(u_field, v_field, sigma, west, dinv, west_coupling, east_coupling):
    shares, strips = lax.axis_size("plane"), lax.axis_size("strip")
    planes_dev, columns, flat_width = u_field.shape
    planes = planes_dev * shares
    rows = flat_width // NODES
    half_cols = columns // 2
    groups = shares // 2
    all_columns = columns * strips
    vmem = pl.BlockSpec(memory_space=pltpu.VMEM)

    onehots = (west[:, :, None] == jnp.arange(rows, dtype=jnp.int32)).astype(jnp.bfloat16)
    sigma_tile = jnp.broadcast_to(jnp.pad(sigma, (0, 128 - planes_dev))[None], (8, 128))
    labels, sigma_tiles = pl.pallas_call(
        label_kernel,
        out_shape=(
            jax.ShapeDtypeStruct((columns, rows, 128), jnp.bfloat16),
            jax.ShapeDtypeStruct((shares, 8, 128), jnp.float32),
        ),
        in_specs=[vmem] * 2,
        out_specs=(vmem, vmem),
        scratch_shapes=[
            pltpu.VMEM((columns, rows, 128), jnp.bfloat16),
            pltpu.VMEM((rows, 128), jnp.bfloat16),
            pltpu.VMEM((strips, rows, 128), jnp.bfloat16),
            pltpu.SemaphoreType.DMA((strips,)),
            pltpu.SemaphoreType.DMA((strips,)),
            pltpu.SemaphoreType.DMA((shares,)),
            pltpu.SemaphoreType.DMA((shares,)),
        ],
        compiler_params=pltpu.CompilerParams(collective_id=0, has_side_effects=True),
    )(onehots, sigma_tile)
    labels = labels[:, :, :rows]
    sigma_all = sigma_tiles[:, 0, :planes_dev].reshape(planes)

    fields = jnp.stack([u_field, v_field]).reshape(2, planes_dev, columns, rows, NODES)
    outgoing = jnp.einsum("grc,fzgrn->gcfzn", labels, fields)
    outgoing = (
        outgoing.reshape(2, half_cols, groups, strips, 2, planes_dev, NODES)
        .transpose(2, 4, 3, 1, 6, 0, 5)
        .reshape(shares * strips, half_cols * NODES, 2 * planes_dev)
    )
    group = lax.axis_index("plane") // 2
    own = lax.dynamic_slice_in_dim(labels, group * strips, strips, 2)
    matrices = jnp.stack([dinv, west_coupling, east_coupling])
    matrices = jnp.einsum("grc,mgre->cmge", own, matrices)
    matrices = lax.all_to_all(matrices, "strip", 0, 0, tiled=True)
    matrices = matrices.reshape(strips, 3 * columns, NODES * NODES)

    (fhi, flo), (bhi, blo) = transform_tables(planes, shares)
    result = pl.pallas_call(
        lambda *refs: chain_kernel(shares, strips, half_cols, *refs),
        out_shape=jax.ShapeDtypeStruct(outgoing.shape, jnp.bfloat16),
        in_specs=[vmem] * 3 + [pl.BlockSpec(memory_space=pltpu.HBM)] * 4,
        out_specs=vmem,
        scratch_shapes=[
            pltpu.VMEM((all_columns, PAD, planes), jnp.float32),
            pltpu.VMEM((all_columns, PAD, 3 * PAD), jnp.bfloat16),
            pltpu.VMEM((all_columns, PAD, 3 * PAD), jnp.bfloat16),
            pltpu.VMEM((all_columns, PAD, 2 * PAD), jnp.bfloat16),
            pltpu.VMEM((strips, 3 * columns, PAD, 128), jnp.float32),
            pltpu.VMEM(outgoing.shape, jnp.bfloat16),
            pltpu.VMEM(outgoing.shape, jnp.bfloat16),
        ]
        + [pltpu.VMEM(table.shape, jnp.bfloat16) for table in (fhi, flo, bhi, blo)]
        + [pltpu.SemaphoreType.DMA((shares * strips,)) for _ in range(4)]
        + [
            pltpu.SemaphoreType.DMA,
            pltpu.SemaphoreType.DMA((4,)),
        ],
        compiler_params=pltpu.CompilerParams(
            vmem_limit_bytes=48 * 1024 * 1024, collective_id=1, has_side_effects=True
        ),
    )(outgoing, sigma_all.reshape(1, planes), matrices, fhi, flo, bhi, blo)

    returned = result.reshape(groups, 2, strips, half_cols, NODES, 2, planes_dev)
    returned = returned.transpose(5, 3, 0, 2, 1, 6, 4).reshape(
        columns, rows, 2, planes_dev, NODES
    )
    outs = jnp.einsum("grc,gcfzn->fzgrn", labels, returned).reshape(
        2, planes_dev, columns, flat_width
    )
    return outs[0], outs[1]


def solution(mesh):
    in_specs = (
        P("plane", "strip", None),
        P("plane", "strip", None),
        P("plane"),
        P("strip", None),
        P("strip", None, None),
        P("strip", None, None),
        P("strip", None, None),
    )
    out_specs = (P("plane", "strip", None), P("plane", "strip", None))
    spread = mesh.shape["plane"] % 2 == 0 and mesh.shape["plane"] * mesh.shape["strip"] == 32
    body = chain_on_device if spread else strip_chain_on_device
    return jax.shard_map(
        body, mesh=mesh, in_specs=in_specs, out_specs=out_specs, check_vma=False
    )
```

```python
import math

import jax
import jax.numpy as jnp
import ml_dtypes
import numpy as np
from jax import lax
from jax.experimental import pallas as pl
from jax.experimental.pallas import tpu as pltpu
from jax.sharding import PartitionSpec as P

NODES = 36


def from_behind(block, axis, distance):
    devices = range(lax.axis_size(axis))
    route = [(i - distance, i) for i in devices if i - distance in devices]
    return lax.ppermute(block, axis, route)


def fourier_tables(count):
    coeff_ids = jnp.arange(count, dtype=jnp.int32)
    plane_ids = jnp.arange(count, dtype=jnp.int32)
    wavenumber = (coeff_ids + 1) // 2
    steps_idx = wavenumber[:, None] * plane_ids[None, :] % count
    angles = steps_idx.astype(jnp.float32) * (2.0 * math.pi / count)
    is_sine = (coeff_ids % 2 == 0) & (coeff_ids > 0)
    basis_rows = jnp.where(is_sine[:, None], jnp.sin(angles), jnp.cos(angles))
    edge_rows = (coeff_ids == 0) | (coeff_ids == count - 1)
    scaling = jnp.where(edge_rows, 1.0 / count, 2.0 / count).astype(jnp.float32)
    return (basis_rows * scaling[:, None], basis_rows.T)


def forward_strip(source, gains, inflow, inverse_blocks, west_blocks, onehots):

    def advance(previous, slices):
        source_col, inverse_col, west_col, onehot = slices
        shifted = jnp.einsum("rs,snl->rnl", onehot, previous, precision=lax.Precision.HIGHEST)
        west_term = jnp.einsum(
            "rij,rjl->ril", west_col.astype(jnp.float32), shifted, precision=lax.Precision.HIGHEST
        )
        reduced = source_col - gains * west_term
        solved = jnp.einsum(
            "rij,rjl->ril",
            inverse_col.astype(jnp.float32),
            reduced,
            precision=lax.Precision.HIGHEST,
        )
        return (solved, reduced)

    return lax.scan(advance, inflow, (source, inverse_blocks, west_blocks, onehots))


def backward_strip(reduced_all, gains, inflow, inverse_blocks, east_blocks, onehots):

    def advance(east_term, slices):
        reduced_col, inverse_col, east_col, onehot = slices
        solved = jnp.einsum(
            "rij,rjl->ril",
            inverse_col.astype(jnp.float32),
            reduced_col - gains * east_term,
            precision=lax.Precision.HIGHEST,
        )
        east_part = jnp.einsum(
            "rij,rjl->ril", east_col.astype(jnp.float32), solved, precision=lax.Precision.HIGHEST
        )
        routed = jnp.einsum("rs,ril->sil", onehot, east_part, precision=lax.Precision.HIGHEST)
        return (routed, solved)

    return lax.scan(
        advance, inflow, (reduced_all, inverse_blocks, east_blocks, onehots), reverse=True
    )


def run_chain(direction, block_count, advance, state, outgoing):
    strip_count = lax.axis_size("strip")
    strip_index = lax.axis_index("strip")
    turn_count = strip_count + block_count - 1

    def one_turn(step_turn, carry):
        incoming = from_behind(carry[0], "strip", direction)
        if direction > 0:
            position = step_turn - strip_index
        else:
            position = step_turn - (strip_count - 1 - strip_index)
        active = (position >= 0) & (position < block_count)
        lane_block = jnp.clip(position, 0, block_count - 1)

        def working(current):
            return advance(incoming, lane_block, current)

        def waiting(current):
            return current

        return lax.cond(active, working, waiting, carry)

    return lax.fori_loop(0, turn_count, one_turn, (outgoing, state))


def strip_chain_on_device(u_field, v_field, sigma, west, dinv, west_coupling, east_coupling):
    planes_dev, columns, flat_width = u_field.shape
    planes = planes_dev * lax.axis_size("plane")
    elem_rows = flat_width // NODES
    forward_table, inverse_table = fourier_tables(planes)
    pieces = (
        lax.all_to_all(u_field, "plane", split_axis=1, concat_axis=0, tiled=True),
        lax.all_to_all(v_field, "plane", split_axis=1, concat_axis=0, tiled=True),
    )
    spec_u, spec_v = tuple(
        (
            jnp.einsum(
                "kz,zcn->kcn",
                forward_table,
                piece.astype(jnp.float32),
                precision=lax.Precision.HIGHEST,
            )
            for piece in pieces
        )
    )
    mode_u, mode_v = (
        lax.all_to_all(spec_u, "plane", split_axis=0, concat_axis=1, tiled=True),
        lax.all_to_all(spec_v, "plane", split_axis=0, concat_axis=1, tiled=True),
    )
    modes_dev = mode_u.shape[0]
    lane_count = 2 * modes_dev
    stacked = (
        jnp.concatenate([mode_u, mode_v], 0)
        .reshape(lane_count, columns, elem_rows, NODES)
        .transpose(1, 2, 3, 0)
    )
    lane_gains = jnp.concatenate([sigma, sigma], 0)
    block_count = 1
    lane_width = lane_count // block_count
    onehots = (west[:, :, None] == jnp.arange(elem_rows, dtype=jnp.int32)[None, None, :]).astype(
        jnp.float32
    )
    inverse_blocks = dinv.reshape(columns, elem_rows, NODES, NODES)
    west_blocks = west_coupling.reshape(columns, elem_rows, NODES, NODES)
    east_blocks = east_coupling.reshape(columns, elem_rows, NODES, NODES)
    edge_zeros = jnp.zeros((elem_rows, NODES, lane_width), jnp.float32)

    def forward_advance(incoming, lane_block, carry):
        last_col, reduced = forward_strip(
            stacked, lane_gains, incoming, inverse_blocks, west_blocks, onehots
        )
        return (last_col, reduced)

    reduced_all = run_chain(1, block_count, forward_advance, jnp.zeros_like(stacked), edge_zeros)[1]

    def backward_advance(incoming, lane_block, carry):
        first_term, solved = backward_strip(
            reduced_all, lane_gains, incoming, inverse_blocks, east_blocks, onehots
        )
        return (first_term, solved)

    solved_all = run_chain(-1, block_count, backward_advance, jnp.zeros_like(stacked), edge_zeros)[
        1
    ]
    result_modes = solved_all.transpose(3, 0, 1, 2).reshape(lane_count, columns, flat_width)
    out_modes_u = result_modes[:modes_dev]
    out_modes_v = result_modes[modes_dev:]
    pieces = (
        lax.all_to_all(out_modes_u, "plane", split_axis=1, concat_axis=0, tiled=True),
        lax.all_to_all(out_modes_v, "plane", split_axis=1, concat_axis=0, tiled=True),
    )
    phys_u, phys_v = tuple(
        (
            jnp.einsum("zk,kcn->zcn", inverse_table, piece, precision=lax.Precision.HIGHEST).astype(
                jnp.bfloat16
            )
            for piece in pieces
        )
    )
    u_out, v_out = (
        lax.all_to_all(phys_u, "plane", split_axis=0, concat_axis=1, tiled=True),
        lax.all_to_all(phys_v, "plane", split_axis=0, concat_axis=1, tiled=True),
    )
    return (u_out, v_out)


PAD = 48


def split_table(table):
    high = table.astype(np.float32).astype(ml_dtypes.bfloat16)
    low = (table - high.astype(np.float64)).astype(ml_dtypes.bfloat16)
    return jnp.asarray(high), jnp.asarray(low)


def transform_tables(count, shares):
    ids = np.arange(count)
    angles = 2.0 * np.pi * (((ids[:, None] + 1) // 2 * ids[None, :]) % count) / count
    is_sine = (ids % 2 == 0) & (ids > 0)
    basis = np.where(is_sine[:, None], np.sin(angles), np.cos(angles))
    scaling = np.where((ids == 0) | (ids == count - 1), 1.0 / count, 2.0 / count)
    forward = basis * scaling[:, None]
    each = count // shares
    to_modes = np.zeros((shares, 2, each, 2, count))
    to_planes = np.zeros((2, count, shares, 2, each))
    for half in range(2):
        to_modes[:, half, :, half, :] = forward.T.reshape(shares, each, count)
        to_planes[half, :, :, half, :] = basis.reshape(count, shares, each)
    return (
        split_table(to_modes.reshape(2 * count, 2 * count)),
        split_table(to_planes.reshape(2 * count, 2 * count)),
    )


def split(value):
    high = value.astype(jnp.bfloat16)
    low = (value - high.astype(jnp.float32)).astype(jnp.bfloat16)
    return high, low


def dot(left, right):
    return jnp.dot(left, right, preferred_element_type=jnp.float32)


def label_kernel(
    onehot_ref, sigma_ref, labels_ref, sigmas_ref,
    local_ref, total_ref, totals_ref, strip_send, strip_recv, plane_send, plane_recv,
):
    columns, rows, _ = onehot_ref.shape
    shares, strips = sigmas_ref.shape[0], totals_ref.shape[0]
    my_share, my_strip = lax.axis_index("plane"), lax.axis_index("strip")

    barrier = pltpu.get_barrier_semaphore()
    for step in range(1, strips):
        pl.semaphore_signal(
            barrier, 1, device_id={"plane": my_share, "strip": (my_strip + step) % strips}
        )
    for step in range(1, shares):
        pl.semaphore_signal(
            barrier, 1, device_id={"plane": (my_share + step) % shares, "strip": my_strip}
        )

    start = (
        lax.broadcasted_iota(jnp.int32, (rows, 128), 0)
        == lax.broadcasted_iota(jnp.int32, (rows, 128), 1)
    ).astype(jnp.bfloat16)
    held = start
    for column in range(columns):
        held = dot(onehot_ref[column], held).astype(jnp.bfloat16)
        local_ref[column] = held
    total_ref[...] = held
    pl.semaphore_wait(barrier, strips + shares - 2)

    def strip_copy(step, slot):
        return pltpu.make_async_remote_copy(
            src_ref=total_ref,
            dst_ref=totals_ref.at[slot],
            send_sem=strip_send.at[step],
            recv_sem=strip_recv.at[slot],
            device_id={"plane": my_share, "strip": (my_strip + step) % strips},
        )

    def plane_copy(step, slot):
        return pltpu.make_async_remote_copy(
            src_ref=sigma_ref,
            dst_ref=sigmas_ref.at[slot],
            send_sem=plane_send.at[step],
            recv_sem=plane_recv.at[slot],
            device_id={"plane": (my_share + step) % shares, "strip": my_strip},
        )

    for step in range(1, strips):
        strip_copy(step, my_strip).start()
    for step in range(1, shares):
        plane_copy(step, my_share).start()
    totals_ref[my_strip] = held
    sigmas_ref[my_share] = sigma_ref[...]
    for step in range(1, strips):
        strip_copy(step, (my_strip + strips - step) % strips).wait_recv()
    before = start
    for strip in range(strips - 1):
        joined = dot(totals_ref[strip][:, :rows], before)
        before = jnp.where(strip < my_strip, joined, before.astype(jnp.float32)).astype(
            jnp.bfloat16
        )
    for column in range(columns):
        labels_ref[column] = dot(local_ref[column][:, :rows], before).astype(jnp.bfloat16)
    for step in range(1, shares):
        plane_copy(step, (my_share + shares - step) % shares).wait_recv()
    for step in range(1, strips):
        strip_copy(step, my_strip).wait_send()
    for step in range(1, shares):
        plane_copy(step, my_share).wait_send()


def pack_kernel(strips, rows_ref, u_ref, v_ref, out_ref, wide_ref, turned_ref):
    planes_dev, columns, flat_width = u_ref.shape
    rows, half_cols = flat_width // NODES, columns // 2
    for field, given in enumerate((u_ref, v_ref)):
        wide_ref[...] = given[...].astype(jnp.float32)
        for place in range(half_cols):
            both = jnp.concatenate([wide_ref[:, place, :], wide_ref[:, half_cols + place, :]], 0)
            turned = both.T
            for row in range(rows):
                turned_ref[field, place, row, :NODES] = turned[row * NODES : (row + 1) * NODES]
    first = lax.broadcasted_iota(jnp.int32, (NODES, 2 * planes_dev), 1) < planes_dev

    def emit(chain, carry):
        for field in range(2):
            pieces = [
                jnp.where(
                    first,
                    turned_ref[field, place, rows_ref[place, chain], :NODES],
                    turned_ref[field, place, rows_ref[half_cols + place, chain], :NODES],
                )
                for place in range(half_cols)
            ]
            device = (chain // strips * 2 + field) * strips + chain % strips
            out_ref[device] = jnp.concatenate(pieces, axis=0).astype(jnp.bfloat16)
        return carry

    lax.fori_loop(0, rows, emit, 0)


def unpack_kernel(strips, chains_ref, given_ref, u_ref, v_ref, wide_ref, turned_ref):
    planes_dev, columns, flat_width = u_ref.shape
    rows, half_cols = flat_width // NODES, columns // 2

    def take(chain, carry):
        for field in range(2):
            device = (chain // strips * 2 + field) * strips + chain % strips
            given = given_ref[device].astype(jnp.float32)
            for place in range(half_cols):
                turned_ref[field, place, chain, :NODES] = given[
                    place * NODES : (place + 1) * NODES
                ]
        return carry

    lax.fori_loop(0, rows, take, 0)
    first = lax.broadcasted_iota(jnp.int32, (NODES, 2 * planes_dev), 1) < planes_dev
    for field, out_ref in enumerate((u_ref, v_ref)):
        for place in range(half_cols):
            pieces = [
                jnp.where(
                    first,
                    turned_ref[field, place, chains_ref[place, row], :NODES],
                    turned_ref[field, place, chains_ref[half_cols + place, row], :NODES],
                )
                for row in range(rows)
            ]
            both = jnp.concatenate(pieces, axis=0).T
            wide_ref[:, place, :] = both[:planes_dev]
            wide_ref[:, half_cols + place, :] = both[planes_dev:]
        out_ref[...] = wide_ref[...].astype(jnp.bfloat16)


def chain_kernel(
    shares, strips, half_cols,
    source_ref, sigma_ref, flat_ref, fhi_in, flo_in, bhi_in, blo_in,
    out_ref,
    x_ref, a_ref, b_ref, inv_ref, square_ref, recv_ref, planes_ref,
    fhi_ref, flo_ref, bhi_ref, blo_ref,
    first_send, first_recv, send_sems, recv_sems, own_sem, table_sems,
):
    my_share, my_strip = lax.axis_index("plane"), lax.axis_index("strip")
    me = my_share * strips + my_strip
    devices = shares * strips
    tables = [
        pltpu.make_async_copy(given, kept, table_sems.at[place])
        for place, (given, kept) in enumerate(
            [(fhi_in, fhi_ref), (flo_in, flo_ref), (bhi_in, bhi_ref), (blo_in, blo_ref)]
        )
    ]
    own_source = pltpu.make_async_copy(source_ref.at[me], recv_ref.at[me], own_sem)
    own_source.start()
    for table in tables:
        table.start()

    barrier = pltpu.get_barrier_semaphore()

    def greet(step, carry):
        other = (me + step) % devices
        pl.semaphore_signal(
            barrier, 1, device_id={"plane": other // strips, "strip": other % strips}
        )
        return carry

    lax.fori_loop(1, devices, greet, 0)

    pl.semaphore_wait(barrier, devices - 1)

    def source_copy(other, slot):
        return pltpu.make_async_remote_copy(
            src_ref=source_ref.at[other],
            dst_ref=recv_ref.at[slot],
            send_sem=first_send.at[other],
            recv_sem=first_recv.at[slot],
            device_id={"plane": other // strips, "strip": other % strips},
        )

    def send_source(step, carry):
        source_copy((me + step) % devices, me).start()
        return carry

    lax.fori_loop(1, devices, send_source, 0)

    def result_copy(share, strip, slot):
        return pltpu.make_async_remote_copy(
            src_ref=planes_ref.at[share * strips + strip],
            dst_ref=out_ref.at[slot],
            send_sem=send_sems.at[share * strips + strip],
            recv_sem=recv_sems.at[slot],
            device_id={"plane": share, "strip": strip},
        )

    columns = x_ref.shape[0]
    modes = x_ref.shape[2]
    per_strip = 2 * half_cols
    square_ref[...] = jnp.zeros_like(square_ref)

    def unflatten(strip, carry):
        flat = flat_ref[strip].astype(jnp.float32)
        for row in range(NODES):
            square_ref[strip, :, row, :NODES] = flat[:, row * NODES : (row + 1) * NODES]
        return carry

    lax.fori_loop(0, strips, unflatten, 0)

    def repeated(count):
        row = lax.broadcasted_iota(jnp.int32, (PAD, count * PAD), 0)
        lane = lax.broadcasted_iota(jnp.int32, (PAD, count * PAD), 1)
        return (row == lane % PAD).astype(jnp.bfloat16)

    lane = lax.broadcasted_iota(jnp.int32, (PAD, 3 * PAD), 1)
    twice, thrice = repeated(2), repeated(3)

    def block(kind, column):
        strip, place = column // per_strip, column % per_strip
        return square_ref[strip, kind * per_strip + place][:, :PAD].astype(jnp.bfloat16)

    def folded(left, right):
        right = dot(right, thrice).astype(jnp.bfloat16)
        high, low = split(dot(left, right))
        return jnp.where(lane < 2 * PAD, high.astype(jnp.float32), low.astype(jnp.float32)).astype(
            jnp.bfloat16
        )

    def prepare(column, carry):
        inverse = block(0, column)
        inv_ref[column] = dot(inverse, twice).astype(jnp.bfloat16)
        a_ref[column] = folded(inverse, block(1, column))
        b_ref[column] = folded(inverse, block(2, jnp.minimum(column + 1, columns - 1)))
        return carry

    lax.fori_loop(0, columns, prepare, 0, unroll=4)

    sigma = jnp.broadcast_to(sigma_ref[...], (PAD, modes))

    def stacked(value):
        high, low = split(value)
        return jnp.concatenate([high, low, high], axis=0)

    def to_modes(step, carry):
        strip = (my_strip + strips - step) % strips
        for share in range(shares):

            @pl.when(share * strips + strip != me)
            def _():
                source_copy(me, share * strips + strip).wait_recv()

        planes = jnp.concatenate(
            [recv_ref[share * strips + strip] for share in range(shares)], axis=1
        )
        coeffs = dot(planes, fhi_ref[...]) + dot(planes, flo_ref[...])
        for half in range(2):
            for place in range(half_cols):
                own = coeffs[place * NODES : (place + 1) * NODES, half * modes : (half + 1) * modes]
                own = jnp.concatenate([own, jnp.zeros((PAD - NODES, modes), jnp.float32)], axis=0)
                high, low = split(own)
                column = (strip * 2 + half) * half_cols + place
                x_ref[column] = dot(inv_ref[column], jnp.concatenate([high, low], axis=0))
        return carry

    own_source.wait()
    for table in tables:
        table.wait()
    lax.fori_loop(0, strips, to_modes, 0)

    def forward(strip, previous):
        for place in range(per_strip):
            column = strip * per_strip + place
            previous = x_ref[column] - sigma * dot(a_ref[column], stacked(previous))
            x_ref[column] = previous
        return previous

    nothing = jnp.zeros((PAD, modes), jnp.float32)
    lax.fori_loop(0, strips, forward, nothing)

    def solve(strip, following):
        solved = [x_ref[strip * per_strip + place] for place in range(per_strip)]
        for place in reversed(range(per_strip)):
            factors = b_ref[strip * per_strip + place]
            following = solved[place] - sigma * dot(factors, stacked(following))
            solved[place] = following
        return solved

    def keep(strip, solved):
        for place in range(per_strip):
            x_ref[strip * per_strip + place] = solved[place]

    def planes_of(strip):
        pieces = []
        for place in range(half_cols):
            first = x_ref[strip * per_strip + place]
            second = x_ref[strip * per_strip + half_cols + place]
            pieces.append(jnp.concatenate([first[:NODES], second[:NODES]], axis=1))
        high, low = split(jnp.concatenate(pieces, axis=0))
        return dot(high, bhi_ref[...]) + dot(low, bhi_ref[...]) + dot(high, blo_ref[...])

    def send(strip, planes):
        width = planes.shape[1] // shares
        for share in range(shares):
            planes_ref[share * strips + strip] = planes[
                :, share * width : (share + 1) * width
            ].astype(jnp.bfloat16)
        for share in range(shares):

            @pl.when(share * strips + strip != me)
            def _():
                result_copy(share, strip, me).start()

    last = solve(strips - 1, nothing)
    keep(strips - 1, last)

    def backward(step, following):
        strip = strips - 1 - step
        planes = planes_of(strip + 1)
        solved = solve(strip, following)
        keep(strip, solved)
        send(strip + 1, planes)
        return solved[0]

    lax.fori_loop(1, strips, backward, last[0])
    send(0, planes_of(0))
    own_copy = pltpu.make_async_copy(planes_ref.at[me], out_ref.at[me], own_sem)
    own_copy.start()
    own_copy.wait()

    def finish(step, carry):
        source = (me + step) % devices
        result_copy(source // strips, source % strips, source).wait_recv()
        result_copy(source // strips, source % strips, me).wait_send()
        source_copy(source, me).wait_send()
        return carry

    lax.fori_loop(1, devices, finish, 0)


def chain_on_device(u_field, v_field, sigma, west, dinv, west_coupling, east_coupling):
    shares, strips = lax.axis_size("plane"), lax.axis_size("strip")
    planes_dev, columns, flat_width = u_field.shape
    planes = planes_dev * shares
    rows = flat_width // NODES
    half_cols = columns // 2
    groups = shares // 2
    all_columns = columns * strips
    vmem = pl.BlockSpec(memory_space=pltpu.VMEM)

    onehots = (west[:, :, None] == jnp.arange(rows, dtype=jnp.int32)).astype(jnp.bfloat16)
    sigma_tile = jnp.broadcast_to(jnp.pad(sigma, (0, 128 - planes_dev))[None], (8, 128))
    labels, sigma_tiles = pl.pallas_call(
        label_kernel,
        out_shape=(
            jax.ShapeDtypeStruct((columns, rows, 128), jnp.bfloat16),
            jax.ShapeDtypeStruct((shares, 8, 128), jnp.float32),
        ),
        in_specs=[vmem] * 2,
        out_specs=(vmem, vmem),
        scratch_shapes=[
            pltpu.VMEM((columns, rows, 128), jnp.bfloat16),
            pltpu.VMEM((rows, 128), jnp.bfloat16),
            pltpu.VMEM((strips, rows, 128), jnp.bfloat16),
            pltpu.SemaphoreType.DMA((strips,)),
            pltpu.SemaphoreType.DMA((strips,)),
            pltpu.SemaphoreType.DMA((shares,)),
            pltpu.SemaphoreType.DMA((shares,)),
        ],
        compiler_params=pltpu.CompilerParams(collective_id=0, has_side_effects=True),
    )(onehots, sigma_tile)
    labels = labels[:, :, :rows]
    sigma_all = sigma_tiles[:, 0, :planes_dev].reshape(planes)

    row_ids = jnp.arange(rows, dtype=jnp.int32)
    whole = labels.astype(jnp.int32)
    rows_of = jnp.sum(whole * row_ids[None, :, None], axis=1)
    chains_of = jnp.sum(whole * row_ids[None, None, :], axis=2)
    smem = pl.BlockSpec(memory_space=pltpu.SMEM)
    spare_space = [
        pltpu.VMEM((planes_dev, columns, flat_width), jnp.float32),
        pltpu.VMEM((2, half_cols, rows, 40, 2 * planes_dev), jnp.float32),
    ]
    outgoing = pl.pallas_call(
        lambda *refs: pack_kernel(strips, *refs),
        out_shape=jax.ShapeDtypeStruct(
            (shares * strips, half_cols * NODES, 2 * planes_dev), jnp.bfloat16
        ),
        in_specs=[smem, vmem, vmem],
        out_specs=vmem,
        scratch_shapes=spare_space,
        compiler_params=pltpu.CompilerParams(vmem_limit_bytes=32 * 1024 * 1024),
    )(rows_of, u_field, v_field)

    group = lax.axis_index("plane") // 2
    own = lax.dynamic_slice_in_dim(labels, group * strips, strips, 2)
    matrices = jnp.stack([dinv, west_coupling, east_coupling])
    matrices = jnp.einsum("grc,mgre->cmge", own, matrices)
    matrices = lax.all_to_all(matrices, "strip", 0, 0, tiled=True)
    matrices = matrices.reshape(strips, 3 * columns, NODES * NODES)

    (fhi, flo), (bhi, blo) = transform_tables(planes, shares)
    result = pl.pallas_call(
        lambda *refs: chain_kernel(shares, strips, half_cols, *refs),
        out_shape=jax.ShapeDtypeStruct(outgoing.shape, jnp.bfloat16),
        in_specs=[vmem] * 3 + [pl.BlockSpec(memory_space=pltpu.HBM)] * 4,
        out_specs=vmem,
        scratch_shapes=[
            pltpu.VMEM((all_columns, PAD, planes), jnp.float32),
            pltpu.VMEM((all_columns, PAD, 3 * PAD), jnp.bfloat16),
            pltpu.VMEM((all_columns, PAD, 3 * PAD), jnp.bfloat16),
            pltpu.VMEM((all_columns, PAD, 2 * PAD), jnp.bfloat16),
            pltpu.VMEM((strips, 3 * columns, PAD, 128), jnp.float32),
            pltpu.VMEM(outgoing.shape, jnp.bfloat16),
            pltpu.VMEM(outgoing.shape, jnp.bfloat16),
        ]
        + [pltpu.VMEM(table.shape, jnp.bfloat16) for table in (fhi, flo, bhi, blo)]
        + [pltpu.SemaphoreType.DMA((shares * strips,)) for _ in range(4)]
        + [
            pltpu.SemaphoreType.DMA,
            pltpu.SemaphoreType.DMA((4,)),
        ],
        compiler_params=pltpu.CompilerParams(
            vmem_limit_bytes=48 * 1024 * 1024, collective_id=1, has_side_effects=True
        ),
    )(outgoing, sigma_all.reshape(1, planes), matrices, fhi, flo, bhi, blo)

    return pl.pallas_call(
        lambda *refs: unpack_kernel(strips, *refs),
        out_shape=(
            jax.ShapeDtypeStruct(u_field.shape, jnp.bfloat16),
            jax.ShapeDtypeStruct(v_field.shape, jnp.bfloat16),
        ),
        in_specs=[smem, vmem],
        out_specs=(vmem, vmem),
        scratch_shapes=spare_space,
        compiler_params=pltpu.CompilerParams(vmem_limit_bytes=32 * 1024 * 1024),
    )(chains_of, result)


def solution(mesh):
    in_specs = (
        P("plane", "strip", None),
        P("plane", "strip", None),
        P("plane"),
        P("strip", None),
        P("strip", None, None),
        P("strip", None, None),
        P("strip", None, None),
    )
    out_specs = (P("plane", "strip", None), P("plane", "strip", None))
    spread = mesh.shape["plane"] % 2 == 0 and mesh.shape["plane"] * mesh.shape["strip"] == 32
    body = chain_on_device if spread else strip_chain_on_device
    return jax.shard_map(
        body, mesh=mesh, in_specs=in_specs, out_specs=out_specs, check_vma=False
    )
```

```python
import math

import jax
import jax.numpy as jnp
import ml_dtypes
import numpy as np
from jax import lax
from jax.experimental import pallas as pl
from jax.experimental.pallas import tpu as pltpu
from jax.sharding import PartitionSpec as P

NODES = 36


def from_behind(block, axis, distance):
    devices = range(lax.axis_size(axis))
    route = [(i - distance, i) for i in devices if i - distance in devices]
    return lax.ppermute(block, axis, route)


def fourier_tables(count):
    coeff_ids = jnp.arange(count, dtype=jnp.int32)
    plane_ids = jnp.arange(count, dtype=jnp.int32)
    wavenumber = (coeff_ids + 1) // 2
    steps_idx = wavenumber[:, None] * plane_ids[None, :] % count
    angles = steps_idx.astype(jnp.float32) * (2.0 * math.pi / count)
    is_sine = (coeff_ids % 2 == 0) & (coeff_ids > 0)
    basis_rows = jnp.where(is_sine[:, None], jnp.sin(angles), jnp.cos(angles))
    edge_rows = (coeff_ids == 0) | (coeff_ids == count - 1)
    scaling = jnp.where(edge_rows, 1.0 / count, 2.0 / count).astype(jnp.float32)
    return (basis_rows * scaling[:, None], basis_rows.T)


def forward_strip(source, gains, inflow, inverse_blocks, west_blocks, onehots):

    def advance(previous, slices):
        source_col, inverse_col, west_col, onehot = slices
        shifted = jnp.einsum("rs,snl->rnl", onehot, previous, precision=lax.Precision.HIGHEST)
        west_term = jnp.einsum(
            "rij,rjl->ril", west_col.astype(jnp.float32), shifted, precision=lax.Precision.HIGHEST
        )
        reduced = source_col - gains * west_term
        solved = jnp.einsum(
            "rij,rjl->ril",
            inverse_col.astype(jnp.float32),
            reduced,
            precision=lax.Precision.HIGHEST,
        )
        return (solved, reduced)

    return lax.scan(advance, inflow, (source, inverse_blocks, west_blocks, onehots))


def backward_strip(reduced_all, gains, inflow, inverse_blocks, east_blocks, onehots):

    def advance(east_term, slices):
        reduced_col, inverse_col, east_col, onehot = slices
        solved = jnp.einsum(
            "rij,rjl->ril",
            inverse_col.astype(jnp.float32),
            reduced_col - gains * east_term,
            precision=lax.Precision.HIGHEST,
        )
        east_part = jnp.einsum(
            "rij,rjl->ril", east_col.astype(jnp.float32), solved, precision=lax.Precision.HIGHEST
        )
        routed = jnp.einsum("rs,ril->sil", onehot, east_part, precision=lax.Precision.HIGHEST)
        return (routed, solved)

    return lax.scan(
        advance, inflow, (reduced_all, inverse_blocks, east_blocks, onehots), reverse=True
    )


def run_chain(direction, block_count, advance, state, outgoing):
    strip_count = lax.axis_size("strip")
    strip_index = lax.axis_index("strip")
    turn_count = strip_count + block_count - 1

    def one_turn(step_turn, carry):
        incoming = from_behind(carry[0], "strip", direction)
        if direction > 0:
            position = step_turn - strip_index
        else:
            position = step_turn - (strip_count - 1 - strip_index)
        active = (position >= 0) & (position < block_count)
        lane_block = jnp.clip(position, 0, block_count - 1)

        def working(current):
            return advance(incoming, lane_block, current)

        def waiting(current):
            return current

        return lax.cond(active, working, waiting, carry)

    return lax.fori_loop(0, turn_count, one_turn, (outgoing, state))


def strip_chain_on_device(u_field, v_field, sigma, west, dinv, west_coupling, east_coupling):
    planes_dev, columns, flat_width = u_field.shape
    planes = planes_dev * lax.axis_size("plane")
    elem_rows = flat_width // NODES
    forward_table, inverse_table = fourier_tables(planes)
    pieces = (
        lax.all_to_all(u_field, "plane", split_axis=1, concat_axis=0, tiled=True),
        lax.all_to_all(v_field, "plane", split_axis=1, concat_axis=0, tiled=True),
    )
    spec_u, spec_v = tuple(
        (
            jnp.einsum(
                "kz,zcn->kcn",
                forward_table,
                piece.astype(jnp.float32),
                precision=lax.Precision.HIGHEST,
            )
            for piece in pieces
        )
    )
    mode_u, mode_v = (
        lax.all_to_all(spec_u, "plane", split_axis=0, concat_axis=1, tiled=True),
        lax.all_to_all(spec_v, "plane", split_axis=0, concat_axis=1, tiled=True),
    )
    modes_dev = mode_u.shape[0]
    lane_count = 2 * modes_dev
    stacked = (
        jnp.concatenate([mode_u, mode_v], 0)
        .reshape(lane_count, columns, elem_rows, NODES)
        .transpose(1, 2, 3, 0)
    )
    lane_gains = jnp.concatenate([sigma, sigma], 0)
    block_count = 1
    lane_width = lane_count // block_count
    onehots = (west[:, :, None] == jnp.arange(elem_rows, dtype=jnp.int32)[None, None, :]).astype(
        jnp.float32
    )
    inverse_blocks = dinv.reshape(columns, elem_rows, NODES, NODES)
    west_blocks = west_coupling.reshape(columns, elem_rows, NODES, NODES)
    east_blocks = east_coupling.reshape(columns, elem_rows, NODES, NODES)
    edge_zeros = jnp.zeros((elem_rows, NODES, lane_width), jnp.float32)

    def forward_advance(incoming, lane_block, carry):
        last_col, reduced = forward_strip(
            stacked, lane_gains, incoming, inverse_blocks, west_blocks, onehots
        )
        return (last_col, reduced)

    reduced_all = run_chain(1, block_count, forward_advance, jnp.zeros_like(stacked), edge_zeros)[1]

    def backward_advance(incoming, lane_block, carry):
        first_term, solved = backward_strip(
            reduced_all, lane_gains, incoming, inverse_blocks, east_blocks, onehots
        )
        return (first_term, solved)

    solved_all = run_chain(-1, block_count, backward_advance, jnp.zeros_like(stacked), edge_zeros)[
        1
    ]
    result_modes = solved_all.transpose(3, 0, 1, 2).reshape(lane_count, columns, flat_width)
    out_modes_u = result_modes[:modes_dev]
    out_modes_v = result_modes[modes_dev:]
    pieces = (
        lax.all_to_all(out_modes_u, "plane", split_axis=1, concat_axis=0, tiled=True),
        lax.all_to_all(out_modes_v, "plane", split_axis=1, concat_axis=0, tiled=True),
    )
    phys_u, phys_v = tuple(
        (
            jnp.einsum("zk,kcn->zcn", inverse_table, piece, precision=lax.Precision.HIGHEST).astype(
                jnp.bfloat16
            )
            for piece in pieces
        )
    )
    u_out, v_out = (
        lax.all_to_all(phys_u, "plane", split_axis=0, concat_axis=1, tiled=True),
        lax.all_to_all(phys_v, "plane", split_axis=0, concat_axis=1, tiled=True),
    )
    return (u_out, v_out)


PAD = 48


def split_table(table):
    high = table.astype(np.float32).astype(ml_dtypes.bfloat16)
    low = (table - high.astype(np.float64)).astype(ml_dtypes.bfloat16)
    return jnp.asarray(high), jnp.asarray(low)


def transform_tables(count, shares):
    ids = np.arange(count)
    angles = 2.0 * np.pi * (((ids[:, None] + 1) // 2 * ids[None, :]) % count) / count
    is_sine = (ids % 2 == 0) & (ids > 0)
    basis = np.where(is_sine[:, None], np.sin(angles), np.cos(angles))
    scaling = np.where((ids == 0) | (ids == count - 1), 1.0 / count, 2.0 / count)
    forward = basis * scaling[:, None]
    each = count // shares
    to_modes = np.zeros((shares, 2, each, 2, count))
    to_planes = np.zeros((2, count, shares, 2, each))
    for half in range(2):
        to_modes[:, half, :, half, :] = forward.T.reshape(shares, each, count)
        to_planes[half, :, :, half, :] = basis.reshape(count, shares, each)
    return (
        split_table(to_modes.reshape(2 * count, 2 * count)),
        split_table(to_planes.reshape(2 * count, 2 * count)),
    )


def split(value):
    high = value.astype(jnp.bfloat16)
    low = (value - high.astype(jnp.float32)).astype(jnp.bfloat16)
    return high, low


def dot(left, right):
    return jnp.dot(left, right, preferred_element_type=jnp.float32)


def label_kernel(
    onehot_ref, sigma_in, labels_ref, sigmas_ref,
    sigma_ref, local_ref, total_ref, totals_ref, strip_send, strip_recv, plane_send, plane_recv,
):
    columns, rows, _ = onehot_ref.shape
    shares, strips = sigmas_ref.shape[0], totals_ref.shape[0]
    my_share, my_strip = lax.axis_index("plane"), lax.axis_index("strip")

    barrier = pltpu.get_barrier_semaphore()
    for step in range(1, strips):
        pl.semaphore_signal(
            barrier, 1, device_id={"plane": my_share, "strip": (my_strip + step) % strips}
        )
    for step in range(1, shares):
        pl.semaphore_signal(
            barrier, 1, device_id={"plane": (my_share + step) % shares, "strip": my_strip}
        )

    sigma_ref[...] = jnp.zeros_like(sigma_ref)
    sigma_ref[0:1, : sigma_in.shape[1]] = sigma_in[...]
    start = (
        lax.broadcasted_iota(jnp.int32, (rows, 128), 0)
        == lax.broadcasted_iota(jnp.int32, (rows, 128), 1)
    ).astype(jnp.bfloat16)
    held = start
    for column in range(columns):
        held = dot(onehot_ref[column], held).astype(jnp.bfloat16)
        local_ref[column] = held
    total_ref[...] = held
    pl.semaphore_wait(barrier, strips + shares - 2)

    def strip_copy(step, slot):
        return pltpu.make_async_remote_copy(
            src_ref=total_ref,
            dst_ref=totals_ref.at[slot],
            send_sem=strip_send.at[step],
            recv_sem=strip_recv.at[slot],
            device_id={"plane": my_share, "strip": (my_strip + step) % strips},
        )

    def plane_copy(step, slot):
        return pltpu.make_async_remote_copy(
            src_ref=sigma_ref,
            dst_ref=sigmas_ref.at[slot],
            send_sem=plane_send.at[step],
            recv_sem=plane_recv.at[slot],
            device_id={"plane": (my_share + step) % shares, "strip": my_strip},
        )

    for step in range(1, strips):
        strip_copy(step, my_strip).start()
    for step in range(1, shares):
        plane_copy(step, my_share).start()
    totals_ref[my_strip] = held
    sigmas_ref[my_share] = sigma_ref[...]
    for step in range(1, strips):
        strip_copy(step, (my_strip + strips - step) % strips).wait_recv()
    before = start
    for strip in range(strips - 1):
        joined = dot(totals_ref[strip][:, :rows], before)
        before = jnp.where(strip < my_strip, joined, before.astype(jnp.float32)).astype(
            jnp.bfloat16
        )
    for column in range(columns):
        labels_ref[column] = dot(local_ref[column][:, :rows], before).astype(jnp.bfloat16)
    for step in range(1, shares):
        plane_copy(step, (my_share + shares - step) % shares).wait_recv()
    for step in range(1, strips):
        strip_copy(step, my_strip).wait_send()
    for step in range(1, shares):
        plane_copy(step, my_share).wait_send()


def pack_kernel(strips, rows_ref, u_ref, v_ref, out_ref, wide_ref, turned_ref):
    planes_dev, columns, flat_width = u_ref.shape
    rows, half_cols = flat_width // NODES, columns // 2
    for field, given in enumerate((u_ref, v_ref)):
        wide_ref[...] = given[...].astype(jnp.float32)
        for place in range(half_cols):
            both = jnp.concatenate([wide_ref[:, place, :], wide_ref[:, half_cols + place, :]], 0)
            turned = both.T
            for row in range(rows):
                turned_ref[field, place, row, :NODES] = turned[row * NODES : (row + 1) * NODES]
    first = lax.broadcasted_iota(jnp.int32, (NODES, 2 * planes_dev), 1) < planes_dev

    def emit(chain, carry):
        for field in range(2):
            pieces = [
                jnp.where(
                    first,
                    turned_ref[field, place, rows_ref[place, chain], :NODES],
                    turned_ref[field, place, rows_ref[half_cols + place, chain], :NODES],
                )
                for place in range(half_cols)
            ]
            device = (chain // strips * 2 + field) * strips + chain % strips
            out_ref[device] = jnp.concatenate(pieces, axis=0).astype(jnp.bfloat16)
        return carry

    lax.fori_loop(0, rows, emit, 0)


def unpack_kernel(strips, chains_ref, given_ref, u_ref, v_ref, wide_ref, turned_ref):
    planes_dev, columns, flat_width = u_ref.shape
    rows, half_cols = flat_width // NODES, columns // 2

    def take(chain, carry):
        for field in range(2):
            device = (chain // strips * 2 + field) * strips + chain % strips
            given = given_ref[device].astype(jnp.float32)
            for place in range(half_cols):
                turned_ref[field, place, chain, :NODES] = given[
                    place * NODES : (place + 1) * NODES
                ]
        return carry

    lax.fori_loop(0, rows, take, 0)
    first = lax.broadcasted_iota(jnp.int32, (NODES, 2 * planes_dev), 1) < planes_dev
    for field, out_ref in enumerate((u_ref, v_ref)):
        for place in range(half_cols):
            pieces = [
                jnp.where(
                    first,
                    turned_ref[field, place, chains_ref[place, row], :NODES],
                    turned_ref[field, place, chains_ref[half_cols + place, row], :NODES],
                )
                for row in range(rows)
            ]
            both = jnp.concatenate(pieces, axis=0).T
            wide_ref[:, place, :] = both[:planes_dev]
            wide_ref[:, half_cols + place, :] = both[planes_dev:]
        out_ref[...] = wide_ref[...].astype(jnp.bfloat16)


def chain_kernel(
    shares, strips, half_cols,
    source_ref, sigma_ref, flat_ref, fhi_in, flo_in, bhi_in, blo_in,
    out_ref,
    x_ref, a_ref, b_ref, inv_ref, square_ref, recv_ref, planes_ref,
    fhi_ref, flo_ref, bhi_ref, blo_ref,
    first_send, first_recv, send_sems, recv_sems, own_sem, table_sems,
):
    my_share, my_strip = lax.axis_index("plane"), lax.axis_index("strip")
    me = my_share * strips + my_strip
    devices = shares * strips
    tables = [
        pltpu.make_async_copy(given, kept, table_sems.at[place])
        for place, (given, kept) in enumerate(
            [(fhi_in, fhi_ref), (flo_in, flo_ref), (bhi_in, bhi_ref), (blo_in, blo_ref)]
        )
    ]
    own_source = pltpu.make_async_copy(source_ref.at[me], recv_ref.at[me], own_sem)
    own_source.start()
    for table in tables:
        table.start()

    barrier = pltpu.get_barrier_semaphore()

    def greet(step, carry):
        other = (me + step) % devices
        pl.semaphore_signal(
            barrier, 1, device_id={"plane": other // strips, "strip": other % strips}
        )
        return carry

    lax.fori_loop(1, devices, greet, 0)

    pl.semaphore_wait(barrier, devices - 1)

    def source_copy(other, slot):
        return pltpu.make_async_remote_copy(
            src_ref=source_ref.at[other],
            dst_ref=recv_ref.at[slot],
            send_sem=first_send.at[other],
            recv_sem=first_recv.at[slot],
            device_id={"plane": other // strips, "strip": other % strips},
        )

    def send_source(step, carry):
        source_copy((me + step) % devices, me).start()
        return carry

    lax.fori_loop(1, devices, send_source, 0)

    def result_copy(share, strip, slot):
        return pltpu.make_async_remote_copy(
            src_ref=planes_ref.at[share * strips + strip],
            dst_ref=out_ref.at[slot],
            send_sem=send_sems.at[share * strips + strip],
            recv_sem=recv_sems.at[slot],
            device_id={"plane": share, "strip": strip},
        )

    columns = x_ref.shape[0]
    modes = x_ref.shape[2]
    per_strip = 2 * half_cols
    square_ref[...] = jnp.zeros_like(square_ref)

    def unflatten(strip, carry):
        flat = flat_ref[strip].astype(jnp.float32)
        for row in range(NODES):
            square_ref[strip, :, row, :NODES] = flat[:, row * NODES : (row + 1) * NODES]
        return carry

    lax.fori_loop(0, strips, unflatten, 0)

    def repeated(count):
        row = lax.broadcasted_iota(jnp.int32, (PAD, count * PAD), 0)
        lane = lax.broadcasted_iota(jnp.int32, (PAD, count * PAD), 1)
        return (row == lane % PAD).astype(jnp.bfloat16)

    lane = lax.broadcasted_iota(jnp.int32, (PAD, 3 * PAD), 1)
    twice, thrice = repeated(2), repeated(3)

    def block(kind, column):
        strip, place = column // per_strip, column % per_strip
        return square_ref[strip, kind * per_strip + place][:, :PAD].astype(jnp.bfloat16)

    def folded(left, right):
        right = dot(right, thrice).astype(jnp.bfloat16)
        high, low = split(dot(left, right))
        return jnp.where(lane < 2 * PAD, high.astype(jnp.float32), low.astype(jnp.float32)).astype(
            jnp.bfloat16
        )

    def prepare(column, carry):
        inverse = block(0, column)
        inv_ref[column] = dot(inverse, twice).astype(jnp.bfloat16)
        a_ref[column] = folded(inverse, block(1, column))
        b_ref[column] = folded(inverse, block(2, jnp.minimum(column + 1, columns - 1)))
        return carry

    lax.fori_loop(0, columns, prepare, 0, unroll=4)

    sigma = jnp.concatenate(
        [sigma_ref[share, 0:1, : modes // shares] for share in range(shares)], axis=1
    )
    sigma = jnp.broadcast_to(sigma, (PAD, modes))

    def stacked(value):
        high, low = split(value)
        return jnp.concatenate([high, low, high], axis=0)

    def to_modes(step, carry):
        strip = (my_strip + strips - step) % strips
        for share in range(shares):

            @pl.when(share * strips + strip != me)
            def _():
                source_copy(me, share * strips + strip).wait_recv()

        planes = jnp.concatenate(
            [recv_ref[share * strips + strip] for share in range(shares)], axis=1
        )
        coeffs = dot(planes, fhi_ref[...]) + dot(planes, flo_ref[...])
        for half in range(2):
            for place in range(half_cols):
                own = coeffs[place * NODES : (place + 1) * NODES, half * modes : (half + 1) * modes]
                own = jnp.concatenate([own, jnp.zeros((PAD - NODES, modes), jnp.float32)], axis=0)
                high, low = split(own)
                column = (strip * 2 + half) * half_cols + place
                x_ref[column] = dot(inv_ref[column], jnp.concatenate([high, low], axis=0))
        return carry

    own_source.wait()
    for table in tables:
        table.wait()
    lax.fori_loop(0, strips, to_modes, 0)

    def forward(strip, previous):
        for place in range(per_strip):
            column = strip * per_strip + place
            previous = x_ref[column] - sigma * dot(a_ref[column], stacked(previous))
            x_ref[column] = previous
        return previous

    nothing = jnp.zeros((PAD, modes), jnp.float32)
    lax.fori_loop(0, strips, forward, nothing)

    def solve(strip, following):
        solved = [x_ref[strip * per_strip + place] for place in range(per_strip)]
        for place in reversed(range(per_strip)):
            factors = b_ref[strip * per_strip + place]
            following = solved[place] - sigma * dot(factors, stacked(following))
            solved[place] = following
        return solved

    def keep(strip, solved):
        for place in range(per_strip):
            x_ref[strip * per_strip + place] = solved[place]

    def planes_of(strip):
        pieces = []
        for place in range(half_cols):
            first = x_ref[strip * per_strip + place]
            second = x_ref[strip * per_strip + half_cols + place]
            pieces.append(jnp.concatenate([first[:NODES], second[:NODES]], axis=1))
        high, low = split(jnp.concatenate(pieces, axis=0))
        return dot(high, bhi_ref[...]) + dot(low, bhi_ref[...]) + dot(high, blo_ref[...])

    def send(strip, planes):
        width = planes.shape[1] // shares
        for share in range(shares):
            planes_ref[share * strips + strip] = planes[
                :, share * width : (share + 1) * width
            ].astype(jnp.bfloat16)
        for share in range(shares):

            @pl.when(share * strips + strip != me)
            def _():
                result_copy(share, strip, me).start()

    last = solve(strips - 1, nothing)
    keep(strips - 1, last)

    def backward(step, following):
        strip = strips - 1 - step
        planes = planes_of(strip + 1)
        solved = solve(strip, following)
        keep(strip, solved)
        send(strip + 1, planes)
        return solved[0]

    lax.fori_loop(1, strips, backward, last[0])
    send(0, planes_of(0))
    own_copy = pltpu.make_async_copy(planes_ref.at[me], out_ref.at[me], own_sem)
    own_copy.start()
    own_copy.wait()

    def finish(step, carry):
        source = (me + step) % devices
        result_copy(source // strips, source % strips, source).wait_recv()
        result_copy(source // strips, source % strips, me).wait_send()
        source_copy(source, me).wait_send()
        return carry

    lax.fori_loop(1, devices, finish, 0)


def chain_on_device(u_field, v_field, sigma, west, dinv, west_coupling, east_coupling):
    shares, strips = lax.axis_size("plane"), lax.axis_size("strip")
    planes_dev, columns, flat_width = u_field.shape
    planes = planes_dev * shares
    rows = flat_width // NODES
    half_cols = columns // 2
    groups = shares // 2
    all_columns = columns * strips
    vmem = pl.BlockSpec(memory_space=pltpu.VMEM)

    onehots = (west[:, :, None] == jnp.arange(rows, dtype=jnp.int32)).astype(jnp.bfloat16)
    labels, sigma_tiles = pl.pallas_call(
        label_kernel,
        out_shape=(
            jax.ShapeDtypeStruct((columns, rows, 128), jnp.bfloat16),
            jax.ShapeDtypeStruct((shares, 8, 128), jnp.float32),
        ),
        in_specs=[vmem] * 2,
        out_specs=(vmem, vmem),
        scratch_shapes=[
            pltpu.VMEM((8, 128), jnp.float32),
            pltpu.VMEM((columns, rows, 128), jnp.bfloat16),
            pltpu.VMEM((rows, 128), jnp.bfloat16),
            pltpu.VMEM((strips, rows, 128), jnp.bfloat16),
            pltpu.SemaphoreType.DMA((strips,)),
            pltpu.SemaphoreType.DMA((strips,)),
            pltpu.SemaphoreType.DMA((shares,)),
            pltpu.SemaphoreType.DMA((shares,)),
        ],
        compiler_params=pltpu.CompilerParams(collective_id=0, has_side_effects=True),
    )(onehots, sigma.reshape(1, planes_dev))
    labels = labels[:, :, :rows]

    row_ids = jnp.arange(rows, dtype=jnp.int32)
    whole = labels.astype(jnp.int32)
    rows_of = jnp.sum(whole * row_ids[None, :, None], axis=1)
    chains_of = jnp.sum(whole * row_ids[None, None, :], axis=2)
    smem = pl.BlockSpec(memory_space=pltpu.SMEM)
    spare_space = [
        pltpu.VMEM((planes_dev, columns, flat_width), jnp.float32),
        pltpu.VMEM((2, half_cols, rows, 40, 2 * planes_dev), jnp.float32),
    ]
    outgoing = pl.pallas_call(
        lambda *refs: pack_kernel(strips, *refs),
        out_shape=jax.ShapeDtypeStruct(
            (shares * strips, half_cols * NODES, 2 * planes_dev), jnp.bfloat16
        ),
        in_specs=[smem, vmem, vmem],
        out_specs=vmem,
        scratch_shapes=spare_space,
        compiler_params=pltpu.CompilerParams(vmem_limit_bytes=32 * 1024 * 1024),
    )(rows_of, u_field, v_field)

    group = lax.axis_index("plane") // 2
    own = lax.dynamic_slice_in_dim(labels, group * strips, strips, 2)
    matrices = jnp.stack([dinv, west_coupling, east_coupling])
    matrices = jnp.einsum("grc,mgre->cmge", own, matrices)
    matrices = lax.all_to_all(matrices, "strip", 0, 0, tiled=True)
    matrices = matrices.reshape(strips, 3 * columns, NODES * NODES)

    (fhi, flo), (bhi, blo) = transform_tables(planes, shares)
    result = pl.pallas_call(
        lambda *refs: chain_kernel(shares, strips, half_cols, *refs),
        out_shape=jax.ShapeDtypeStruct(outgoing.shape, jnp.bfloat16),
        in_specs=[vmem] * 3 + [pl.BlockSpec(memory_space=pltpu.HBM)] * 4,
        out_specs=vmem,
        scratch_shapes=[
            pltpu.VMEM((all_columns, PAD, planes), jnp.float32),
            pltpu.VMEM((all_columns, PAD, 3 * PAD), jnp.bfloat16),
            pltpu.VMEM((all_columns, PAD, 3 * PAD), jnp.bfloat16),
            pltpu.VMEM((all_columns, PAD, 2 * PAD), jnp.bfloat16),
            pltpu.VMEM((strips, 3 * columns, PAD, 128), jnp.float32),
            pltpu.VMEM(outgoing.shape, jnp.bfloat16),
            pltpu.VMEM(outgoing.shape, jnp.bfloat16),
        ]
        + [pltpu.VMEM(table.shape, jnp.bfloat16) for table in (fhi, flo, bhi, blo)]
        + [pltpu.SemaphoreType.DMA((shares * strips,)) for _ in range(4)]
        + [
            pltpu.SemaphoreType.DMA,
            pltpu.SemaphoreType.DMA((4,)),
        ],
        compiler_params=pltpu.CompilerParams(
            vmem_limit_bytes=60 * 1024 * 1024, collective_id=1, has_side_effects=True
        ),
    )(outgoing, sigma_tiles, matrices, fhi, flo, bhi, blo)

    return pl.pallas_call(
        lambda *refs: unpack_kernel(strips, *refs),
        out_shape=(
            jax.ShapeDtypeStruct(u_field.shape, jnp.bfloat16),
            jax.ShapeDtypeStruct(v_field.shape, jnp.bfloat16),
        ),
        in_specs=[smem, vmem],
        out_specs=(vmem, vmem),
        scratch_shapes=spare_space,
        compiler_params=pltpu.CompilerParams(vmem_limit_bytes=32 * 1024 * 1024),
    )(chains_of, result)


def solution(mesh):
    in_specs = (
        P("plane", "strip", None),
        P("plane", "strip", None),
        P("plane"),
        P("strip", None),
        P("strip", None, None),
        P("strip", None, None),
        P("strip", None, None),
    )
    out_specs = (P("plane", "strip", None), P("plane", "strip", None))
    spread = mesh.shape["plane"] % 2 == 0 and mesh.shape["plane"] * mesh.shape["strip"] == 32
    body = chain_on_device if spread else strip_chain_on_device
    return jax.shard_map(
        body, mesh=mesh, in_specs=in_specs, out_specs=out_specs, check_vma=False
    )
```
